512 devices in a mesh: ops: 32 (over x, z_hi, core), sec: 16 (over z_lo, y).
Axes of the slice: x: 4, y: 4, z: 16 (z_hi: 4, z_lo: 4; z = z_hi * 4 + z_lo), core: 2. Of those that a mesh axis runs over, the one named last changes fastest.
Arguments:
- wave_t: bfloat16 [16, 512, 512], P(None, 'sec'), may hold values from -6 to 6
- left_ops: bfloat16 [96, 512, 512], P('ops'), may hold values from -0.25 to 0.25
- right_ops: bfloat16 [96, 512, 512], P('ops'), may hold values from -0.02734375 to 0.02734375
- pattern: int32 [96, 16], P('ops'), may hold values from 0 to 15
- sector_size: int32 [16], replicated, may hold values from 128 to 512, as said below
Outputs:
- first_image: bfloat16 [16, 512, 512], P(None, 'sec')
- second_image: bfloat16 [16, 512, 512], P(None, 'sec')
The draws below stay inside these ranges and needn't reach their ends.
Inputs may be any that keep to these rules, and one draw needn't show every extreme that they name: `sector_size`: multiples of 128; the largest is exactly 512 and the smallest exactly 128.
All inputs are finite; a program needn't handle non-finite values.
Results may differ from the reference program's by a relative error of at most 0.009.
Values may be sent and summed in bfloat16 or wider, within the bound.
A program may use at most 64 MiB of HBM per device.

```python
import jax
import jax.numpy as jnp
from jax import lax

B = 512
NB = 16
TERMS = 96


def draw_sector_size(key, part):
    key = jax.random.fold_in(key, 7)
    units = jax.random.randint(jax.random.fold_in(key, 1), (NB,), 1, B // 128 + 1)
    where_full = jax.random.randint(jax.random.fold_in(key, 2), (), 0, NB)
    offset = jax.random.randint(jax.random.fold_in(key, 3), (), 1, NB)
    where_small = (where_full + offset) % NB
    places = jnp.arange(NB)
    units = jnp.where(places == where_full, B // 128, units)
    units = jnp.where(places == where_small, 1, units)
    return (units * 128).astype(jnp.int32)


def with_ends(array, rng, smallest, high):
    longest = array.shape.index(max(array.shape))
    spots = []
    for shift in (0, 1):
        where = [jax.random.randint(jax.random.fold_in(rng, axis), (), 0, length) for axis, length in enumerate(array.shape)]
        where[longest] = (where[longest] + shift) % array.shape[longest]
        spots.append(tuple(where))
    return array.at[spots[0]].set(smallest).at[spots[1]].set(high)


def levels(own_key, extent, pieces, low, top_value):
    def one(axis_at, blocks):
        heights = jax.random.uniform(jax.random.fold_in(jax.random.fold_in(own_key, 6), axis_at), (blocks,), jnp.float32, low / len(pieces), top_value / len(pieces))
        return jnp.repeat(jnp.exp(heights), extent[axis_at] // blocks).reshape((-1,) + (1,) * (len(extent) - axis_at - 1))

    gain = one(*pieces[0])
    for cut in pieces[1:]:
        gain = gain * one(*cut)
    return gain


def centred(rng, shape, spread, limit, shards=(), kind=jnp.bfloat16):
    result = spread * jax.random.normal(rng, shape, jnp.float32)
    if shards:
        result = result * levels(rng, shape, shards, -0.22, 0.18)
    return jnp.clip(result, -limit, limit).astype(kind)


def setup_inputs(seed: int = 0) -> dict:
    key_list = jax.random.split(jax.random.key(seed), 6)
    return {
        "wave_t": centred(key_list[0], (NB, B, B), 1.0, 6.0, ((1, 16),)),
        "left_ops": centred(key_list[1], (TERMS, B, B), B ** -0.5, 0.25, ((0, 32),)),
        "right_ops": centred(key_list[2], (TERMS, B, B), (B * TERMS) ** -0.5, 0.02734375, ((0, 32),)),
        "pattern": with_ends(jax.random.randint(key_list[3], (TERMS, NB), 0, NB), jax.random.fold_in(key_list[3], 1), 0, NB - 1).astype(jnp.int32),
        "sector_size": draw_sector_size(jax.random.fold_in(key_list[5], 71), 0),
    }


def masked(values, sector_size):
    inside = jnp.arange(values.shape[1])[None, :] < sector_size[:, None]
    keep = inside[:, :, None] & inside[:, None, :]
    return jnp.where(keep, values, jnp.zeros((), values.dtype))


def apply_hamiltonian(vector, left_ops, right_ops, pattern, sector_size):
    def one_term(total, term):
        source = jnp.take(vector, pattern[term], axis=0).astype(jnp.float32)
        left = jnp.einsum('ij,bjc->bic', left_ops[term].astype(jnp.float32), source)
        left = left.astype(jnp.bfloat16).astype(jnp.float32)
        total = total + jnp.einsum('bic,jc->bij', left, right_ops[term].astype(jnp.float32))
        return total, None

    start = jnp.zeros(vector.shape, jnp.float32)
    total, unused = lax.scan(one_term, start, jnp.arange(pattern.shape[0]).astype(jnp.int32))
    return masked(total, sector_size).astype(jnp.bfloat16)


def reference(wave_t, left_ops, right_ops, pattern, sector_size):
    psi = masked(jnp.swapaxes(wave_t, 1, 2), sector_size)
    first_image = apply_hamiltonian(psi, left_ops, right_ops, pattern, sector_size)
    second_image = apply_hamiltonian(first_image, left_ops, right_ops, pattern, sector_size)
    return first_image, second_image
```

```python
import jax
import jax.numpy as jnp
from jax import lax
from jax.experimental import pallas as pl
from jax.experimental.pallas import tpu as pltpu
from jax.sharding import PartitionSpec as P

MESH = pl.DeviceIdType.MESH
BF = jnp.bfloat16
F32 = jnp.float32
NT = (((1,), (1,)), ((), ()))
NN = (((1,), (0,)), ((), ()))


def dot(a, b, dims):
    return lax.dot_general(a, b, dims, preferred_element_type=F32)


def kernel(
    wave, lops, rops, pat, sizes, out1, out2,
    wbuf, lf, rf, rsel, lsel, va, vb, mid,
    s0s1, s0r1, s01, r1y1, r1x1, t11, t21, r2x1, r2y1, wf1, wb1, r31, f1,
    s0s2, s0r2, s02, r1y2, r1x2, t12, t22, r2x2, r2y2, wf2, wb2, r32, f2,
    obuf, lsem, ssem, rsem,
):
    ops, sec = lax.axis_index("ops"), lax.axis_index("sec")
    x, zh, c = ops // 8, (ops // 2) % 4, ops % 2
    zl, y = sec // 4, sec % 4
    z = zh * 4 + zl

    def to_x(d):
        return {"ops": ((x + d) % 4 * 4 + zh) * 2 + c, "sec": sec}

    def to_y(d):
        return {"ops": ops, "sec": zl * 4 + (y + d) % 4}

    def to_z(d):
        w = (z + d + 16) % 16
        return {"ops": (x * 4 + w // 4) * 2 + c, "sec": w % 4 * 4 + y}

    def to_zz(dh, dl):
        return {"ops": (x * 4 + (zh + dh) % 4) * 2 + c, "sec": (zl + dl) % 4 * 4 + y}

    other = {"ops": ops + 1 - 2 * c, "sec": sec}

    sent = []
    count = [0]

    def copies(n):
        first = count[0]
        count[0] += n
        return first

    def send(src, dst, index, device):
        cp = pltpu.make_async_remote_copy(
            src_ref=src, dst_ref=dst, send_sem=ssem.at[index], recv_sem=rsem.at[index],
            device_id=device, device_id_type=MESH,
        )
        cp.start()
        sent.append(cp)

    def arrived(ref, index):
        pltpu.make_async_copy(ref, ref, rsem.at[index]).wait()

    load_w = pltpu.make_async_copy(wave, wbuf, lsem.at[0])
    load_r = pltpu.make_async_copy(rops, rf, lsem.at[1])
    load_l = pltpu.make_async_copy(lops, lf, lsem.at[2])
    load_w.start()
    load_r.start()
    load_l.start()
    partners = [other] + [to_y(d) for d in (1, 2, 3)] + [to_x(d) for d in (1, 2, 3)] + [to_z(d) for d in range(1, 16)]
    barrier = pltpu.get_barrier_semaphore()
    for device in partners:
        pl.semaphore_signal(barrier, inc=1, device_id=device, device_id_type=MESH)

    load_w.wait()
    row = lax.broadcasted_iota(jnp.int32, (4, 16, 512), 0) % 2 * 16 + lax.broadcasted_iota(jnp.int32, (4, 16, 512), 1)
    row = row + (zl * 128 + y * 32)
    col = lax.broadcasted_iota(jnp.int32, (4, 16, 512), 2)
    part = lax.broadcasted_iota(jnp.int32, (4, 16, 512), 0) // 2
    edge = jnp.maximum(row, col)

    def mask_wave(k, carry):
        cc, xx = k // 4, k % 4
        size = jnp.where(part == 0, sizes[2 * k], sizes[2 * k + 1])
        va[zl, cc, xx] = jnp.where(edge < size, wbuf[cc, xx].astype(F32), 0.0).astype(BF)
        return carry

    lax.fori_loop(0, 8, mask_wave, 0)
    pl.semaphore_wait(barrier, len(partners))

    z_of = [zl, (zl + 3) % 4, (zl + 1) % 4, (zl + 2) % 4]


    def gather(v, whole_slab):
        a1, b1, a2, b2, cx = copies(4), copies(3), copies(12), copies(16), copies(4)
        mine = v.at[zl, c, x]
        low = mine.at[pl.ds(0, 2)]
        send(low, low, a1, to_z(1))
        send(low, low, a1 + 1, to_z(-1))
        send(mine.at[0], mine.at[0], a1 + 2, to_z(2))
        send(mine.at[1], mine.at[1], a1 + 3, to_z(-2))

        def b2_send(xx, k):
            high = v.at[zl, c, xx, pl.ds(2, 2)]
            send(high, high, b2 + 4 * k, to_z(1))
            send(high, high, b2 + 4 * k + 1, to_z(-1))
            send(v.at[zl, c, xx, 2], v.at[zl, c, xx, 2], b2 + 4 * k + 2, to_z(2))
            send(v.at[zl, c, xx, 3], v.at[zl, c, xx, 3], b2 + 4 * k + 3, to_z(-2))

        def a2_send(k):
            block = v.at[z_of[k], c, x, pl.ds(0, 2)]
            for d in (1, 2, 3):
                send(block, block, a2 + 3 * k + d - 1, to_x(d))

        def a1_wait(k):
            block = v.at[z_of[k], c, x]
            if k < 3:
                arrived(block.at[pl.ds(0, 2)], a1 + k - 1)
            else:
                arrived(block.at[0], a1 + 2)
                arrived(block.at[1], a1 + 3)

        x_of = [x, (x + 3) % 4, (x + 1) % 4, (x + 2) % 4]
        step = [0, 1, 3, 2]
        if whole_slab:
            for k in range(4):
                b2_send(x_of[k], k)
        else:
            high = mine.at[pl.ds(2, 2)]
            for d in (1, 2, 3):
                send(high, high, b1 + d - 1, to_x(d))
            a2_send(0)
            b2_send(x, 0)
        for k in (1, 2, 3):
            if not whole_slab:
                arrived(v.at[zl, c, x_of[k], pl.ds(2, 2)], b1 + step[k] - 1)
                b2_send(x_of[k], k)
            a1_wait(k)
            a2_send(k)
        for k in range(4):
            if k == 0 and whole_slab:
                continue
            for m in (1, 2, 3):
                arrived(v.at[z_of[k], c, x_of[m], pl.ds(0, 2)], a2 + 3 * k + step[m] - 1)
            if k > 0:
                for m in range(4):
                    block = v.at[z_of[k], c, x_of[m]]
                    if k < 3:
                        arrived(block.at[pl.ds(2, 2)], b2 + 4 * m + k - 1)
                    else:
                        arrived(block.at[2], b2 + 4 * m + 2)
                        arrived(block.at[3], b2 + 4 * m + 3)
            send(v.at[z_of[k], c], v.at[z_of[k], c], cx + k, other)

        def other_core():
            for k in range(4):
                if k == 0 and whole_slab:
                    continue
                arrived(v.at[z_of[k], 1 - c], cx + k)

        return other_core

    def reduce(pair, tr, tc, s0s, s0r, s0, r1y, r1x, t1, t2, r2x, r2y, wf, wb, r3):
        p0, py, px, qx, qy, p3 = copies(4), copies(12), copies(3), copies(3), copies(3), copies(3)
        for k, d in enumerate((1, 2, 3, 0)):
            xx = (x + d) % 4
            s0s[xx] = pair(1 - c, xx).astype(BF)
            send(s0s.at[xx], s0r.at[xx], p0 + k, other)
        for k, d in enumerate((1, 2, 3, 0)):
            xx = (x + d) % 4
            total = pair(c, xx)
            arrived(s0r.at[xx], p0 + k)
            s0[xx] = (total + s0r[xx].astype(F32)).astype(BF)
            if d:
                send(s0.at[xx, 1], r1x.at[d - 1], px + d - 1, to_x(d))
            for e in (1, 2, 3):
                send(s0.at[xx, 0, (y + e) % 4], r1y.at[e - 1, xx], py + 3 * k + e - 1, to_y(e))

        def sum_t1(k, xx):
            total = s0[xx, 0, y].astype(F32)
            for e in (1, 2, 3):
                arrived(r1y.at[e - 1, xx], py + 3 * k + e - 1)
                total = total + r1y[e - 1, xx].astype(F32)
            return total

        def sum_t2(q):
            total = s0[x, 1, q].astype(F32)
            for d in (1, 2, 3):
                total = total + r1x[d - 1, q].astype(F32)
            return total

        for k, d in enumerate((1, 2, 3)):
            xx = (x + d) % 4
            t1[xx] = sum_t1(k, xx).astype(BF)
            send(t1.at[xx], r2x.at[d - 1], qx + d - 1, to_x(d))
        for d in (1, 2, 3):
            arrived(r1x.at[d - 1], px + d - 1)
        for e in (1, 2, 3):
            q = (y + e) % 4
            t2[q] = sum_t2(q).astype(BF)
            send(t2.at[q], r2y.at[e - 1], qy + e - 1, to_y(e))
        w0 = sum_t1(3, x)
        w1 = sum_t2(y)
        for d in (1, 2, 3):
            arrived(r2x.at[d - 1], qx + d - 1)
            w0 = w0 + r2x[d - 1].astype(F32)
        for d in (1, 2, 3):
            arrived(r2y.at[d - 1], qy + d - 1)
            w1 = w1 + r2y[d - 1].astype(F32)
        half = tr // 2
        for h, part_sum in enumerate((w0[:half], w0[half:], w1[:half], w1[half:])):
            wf[h] = part_sum
            wb[h] = part_sum.astype(BF)
        for d in (1, 2, 3):
            send(wb.at[(zh + d) % 4], r3.at[d - 1], p3 + d - 1, to_z(4 * d))
        total = wf[zh]
        for d in (1, 2, 3):
            arrived(r3.at[d - 1], p3 + d - 1)
            total = total + r3[d - 1].astype(F32)
        return total

    def pick(shape, kdim):
        k = lax.broadcasted_iota(jnp.int32, shape, kdim)
        m = lax.broadcasted_iota(jnp.int32, shape, 1 - kdim)
        return jnp.where(k == m // 32 * 128 + y * 32 + m % 32, 1.0, 0.0).astype(BF)

    other_core = gather(va, True)
    load_r.wait()
    load_l.wait()
    pick_t = pick((128, 512), 1)
    for t in range(3):
        rsel[pl.ds(128 * t, 128)] = dot(pick_t, rf[t], NT).astype(BF)
    pick_n = pick((512, 128), 0)
    for t in range(3):
        chosen = dot(lf[t], pick_n, NN).astype(BF)
        for zz in range(4):
            for q in range(4):
                for rh in range(2):
                    a = zz * 128 + q * 32 + rh * 16
                    b = q * 128 + rh * 64 + zz * 16
                    lsel[b : b + 16, 128 * t : 128 * t + 128] = chosen[a : a + 16]

    def left_half(cc):
        lrows = jnp.concatenate([lf[t, pl.ds(zl * 128, 128)] for t in range(3)], axis=0)

        def body(xx, carry):
            src = [va[:, cc, xx, pl.ds(2 * bp, 2)].reshape(128, 512) for bp in range(2)]
            res = dot(lrows, jnp.concatenate(src, axis=0), NT).astype(BF)
            for t in range(3):
                for bp in range(2):
                    mid[t, cc * 8 + xx * 2 + bp] = res[128 * t : 128 * t + 128, 128 * bp : 128 * bp + 128]
            return carry

        lax.fori_loop(0, 4, body, 0)

    left_half(c)
    other_core()
    left_half(1 - c)

    def pair1(cc, xx):
        rows = []
        for bp in range(2):
            b = cc * 8 + xx * 2 + bp
            rows.append(jnp.concatenate([mid[t, pat[t, b]] for t in range(3)], axis=1))
        res = dot(jnp.concatenate(rows, axis=0), rsel[...], NN)
        return res.reshape(2, 4, 32, 512)

    total = reduce(pair1, 32, 512, s0s1, s0r1, s01, r1y1, r1x1, t11, t21, r2x1, r2y1, wf1, wb1, r31)
    b_mine = c * 8 + x * 2 + zh // 2
    size = sizes[b_mine]
    rr = lax.broadcasted_iota(jnp.int32, (16, 512), 0) + (zl * 128 + y * 32 + zh % 2 * 16)
    cc_ = lax.broadcasted_iota(jnp.int32, (16, 512), 1)
    piece = jnp.where(jnp.maximum(rr, cc_) < size, total, 0.0).astype(BF)
    f1[...] = piece
    g1 = copies(3)
    for d in (1, 2, 3):
        send(f1, vb.at[zl, c, x, zh], g1 + d - 1, to_z(4 * d))
    vb[zl, c, x, zh] = piece
    for d in (1, 2, 3):
        arrived(vb.at[zl, c, x, (zh + 4 - d) % 4], g1 + d - 1)

    other_core = gather(vb, False)

    def right_half(cc):
        rrows = jnp.concatenate([rf[t, pl.ds(zl * 128, 128)] for t in range(3)], axis=0)

        def body(xx, carry):
            src = [vb[:, cc, xx, pl.ds(2 * bp, 2)].reshape(128, 512) for bp in range(2)]
            res = dot(jnp.concatenate(src, axis=0), rrows, NT).astype(BF)
            for t in range(3):
                for bp in range(2):
                    mid[t, cc * 8 + xx * 2 + bp] = res[128 * bp : 128 * bp + 128, 128 * t : 128 * t + 128]
            return carry

        lax.fori_loop(0, 4, body, 0)

    right_half(c)
    other_core()
    store1 = pltpu.make_async_copy(vb.at[zl], out1, lsem.at[3])
    store1.start()
    right_half(1 - c)

    def pair2(cc, xx):
        cols = []
        for bp in range(2):
            b = cc * 8 + xx * 2 + bp
            cols.append(jnp.concatenate([mid[t, pat[t, b]] for t in range(3)], axis=0))
        res = dot(lsel[...], jnp.concatenate(cols, axis=1), NN)
        return jnp.stack([res[:, :128].reshape(4, 128, 128), res[:, 128:].reshape(4, 128, 128)])

    total = reduce(pair2, 128, 128, s0s2, s0r2, s02, r1y2, r1x2, t12, t22, r2x2, r2y2, wf2, wb2, r32)
    total = total.reshape(4, 16, 128)
    rr = lax.broadcasted_iota(jnp.int32, (4, 16, 128), 0) * 128 + lax.broadcasted_iota(jnp.int32, (4, 16, 128), 1)
    rr = rr + (y * 32 + zh % 2 * 16)
    cc_ = lax.broadcasted_iota(jnp.int32, (4, 16, 128), 2) + zl * 128
    piece = jnp.where(jnp.maximum(rr, cc_) < size, total, 0.0).astype(BF)
    f2[...] = piece
    g2 = copies(16)
    here = obuf.at[c, x, zh, :, pl.ds(pl.multiple_of(zl * 128, 128), 128)]
    own = pltpu.make_async_copy(f2.at[zl], here, lsem.at[4])
    own.start()
    for dl in range(4):
        for dh in range(4):
            if dl or dh:
                send(f2.at[(zl + dl) % 4], here, g2 + 4 * dl + dh, to_zz(dh, dl))
    own.wait()
    for dl in range(4):
        for dh in range(4):
            if dl or dh:
                zz = (zl + 4 - dl) % 4
                there = obuf.at[c, x, (zh + 4 - dh) % 4, :, pl.ds(pl.multiple_of(zz * 128, 128), 128)]
                arrived(there, g2 + 4 * dl + dh)
    gx, gc = copies(3), copies(4)
    for d in (1, 2, 3):
        send(obuf.at[c, x], obuf.at[c, x], gx + d - 1, to_x(d))
    send(obuf.at[c, x], obuf.at[c, x], gc, other)
    for d in (1, 3, 2):
        xx = (x + 4 - d) % 4
        arrived(obuf.at[c, xx], gx + d - 1)
        send(obuf.at[c, xx], obuf.at[c, xx], gc + d, other)
    for d in range(4):
        arrived(obuf.at[1 - c, (x + 4 - d) % 4], gc + d)
    store2 = pltpu.make_async_copy(obuf, out2, lsem.at[5])
    store2.start()
    for cp in sent:
        cp.wait_send()
    store1.wait()
    store2.wait()


N_COPIES = 39 + 28 + 3 + 39 + 28 + 16 + 7


def on_device(wave_t, left_ops, right_ops, pattern, sector_size):
    def stage(tr, tc):
        return [
            pltpu.VMEM((4, 2, 4, tr, tc), BF),
            pltpu.VMEM((4, 2, 4, tr, tc), BF),
            pltpu.VMEM((4, 2, 4, tr, tc), BF),
            pltpu.VMEM((3, 4, tr, tc), BF),
            pltpu.VMEM((3, 4, tr, tc), BF),
            pltpu.VMEM((4, tr, tc), BF),
            pltpu.VMEM((4, tr, tc), BF),
            pltpu.VMEM((3, tr, tc), BF),
            pltpu.VMEM((3, tr, tc), BF),
            pltpu.VMEM((4, tr // 2, tc), F32),
            pltpu.VMEM((4, tr // 2, tc), BF),
            pltpu.VMEM((3, tr // 2, tc), BF),
        ]

    hbm = pl.BlockSpec(memory_space=pl.ANY)
    smem = pl.BlockSpec(memory_space=pltpu.SMEM)
    out = jax.ShapeDtypeStruct((2, 4, 4, 16, 512), BF)
    first, second = pl.pallas_call(
        kernel,
        out_shape=(out, out),
        in_specs=[hbm, hbm, hbm, smem, smem],
        out_specs=(hbm, hbm),
        scratch_shapes=[
            pltpu.VMEM((2, 4, 4, 16, 512), BF),
            pltpu.VMEM((3, 512, 512), BF),
            pltpu.VMEM((3, 512, 512), BF),
            pltpu.VMEM((384, 512), BF),
            pltpu.VMEM((512, 384), BF),
            pltpu.VMEM((4, 2, 4, 4, 16, 512), BF),
            pltpu.VMEM((4, 2, 4, 4, 16, 512), BF),
            pltpu.VMEM((3, 16, 128, 128), BF),
            *stage(32, 512),
            pltpu.VMEM((16, 512), BF),
            *stage(128, 128),
            pltpu.VMEM((4, 16, 128), BF),
            pltpu.VMEM((2, 4, 4, 16, 512), BF),
            pltpu.SemaphoreType.DMA((6,)),
            pltpu.SemaphoreType.DMA((N_COPIES,)),
            pltpu.SemaphoreType.DMA((N_COPIES,)),
        ],
        compiler_params=pltpu.CompilerParams(
            collective_id=0, has_side_effects=True, vmem_limit_bytes=48 * 2**20
        ),
        name="hamiltonian",
    )(wave_t.reshape(2, 4, 4, 16, 512), left_ops, right_ops, pattern, sector_size)
    return first.reshape(16, 32, 512), second.reshape(16, 32, 512)


def solution(mesh):
    return jax.shard_map(
        on_device,
        mesh=mesh,
        in_specs=(
            P(None, "sec", None),
            P("ops", None, None),
            P("ops", None, None),
            P("ops", None),
            P(),
        ),
        out_specs=(P(None, "sec", None), P(None, "sec", None)),
        check_vma=False,
    )
```

```python
import jax
import jax.numpy as jnp
from jax import lax
from jax.experimental import pallas as pl
from jax.experimental.pallas import tpu as pltpu
from jax.sharding import PartitionSpec as P

MESH = pl.DeviceIdType.MESH
BF = jnp.bfloat16
F32 = jnp.float32
NT = (((1,), (1,)), ((), ()))
NN = (((1,), (0,)), ((), ()))


def dot(a, b, dims):
    return lax.dot_general(a, b, dims, preferred_element_type=F32)


def kernel(
    wave, lops, rops, pat, sizes, out1, out2,
    wbuf, lf, rf, rsel, lsel, va, vb, mid,
    s0s1, s0r1, s01, r1y1, r1x1, t11, t21, r2x1, r2y1, wf1, wb1, r31, f1,
    s0s2, s0r2, s02, r1y2, r1x2, t12, t22, r2x2, r2y2, wf2, wb2, r32, f2,
    obuf, lsem, ssem, rsem, relay,
):
    ops, sec = lax.axis_index("ops"), lax.axis_index("sec")
    x, zh, c = ops // 8, (ops // 2) % 4, ops % 2
    zl, y = sec // 4, sec % 4
    z = zh * 4 + zl

    def to_x(d):
        return {"ops": ((x + d) % 4 * 4 + zh) * 2 + c, "sec": sec}

    def to_y(d):
        return {"ops": ops, "sec": zl * 4 + (y + d) % 4}

    def to_z(d):
        w = (z + d + 16) % 16
        return {"ops": (x * 4 + w // 4) * 2 + c, "sec": w % 4 * 4 + y}

    def to_zz(dh, dl):
        return {"ops": (x * 4 + (zh + dh) % 4) * 2 + c, "sec": (zl + dl) % 4 * 4 + y}

    other = {"ops": ops + 1 - 2 * c, "sec": sec}

    sent = []
    count = [0]

    def copies(n):
        first = count[0]
        count[0] += n
        return first

    def send(src, dst, index, device):
        cp = pltpu.make_async_remote_copy(
            src_ref=src, dst_ref=dst, send_sem=ssem.at[index], recv_sem=rsem.at[index],
            device_id=device, device_id_type=MESH,
        )
        cp.start()
        sent.append(cp)

    def arrived(ref, index):
        pltpu.make_async_copy(ref, ref, rsem.at[index]).wait()

    load_w = pltpu.make_async_copy(wave, wbuf, lsem.at[0])
    load_r = pltpu.make_async_copy(rops, rf, lsem.at[1])
    load_l = pltpu.make_async_copy(lops, lf, lsem.at[2])
    load_w.start()
    load_r.start()
    load_l.start()
    partners = [other] + [to_y(d) for d in (1, 2, 3)] + [to_x(d) for d in (1, 2, 3)] + [to_z(d) for d in (1, 2, -2, -1)]
    barrier = pltpu.get_barrier_semaphore()
    for device in partners:
        pl.semaphore_signal(barrier, inc=1, device_id=device, device_id_type=MESH)

    load_w.wait()
    row = lax.broadcasted_iota(jnp.int32, (4, 16, 512), 0) % 2 * 16 + lax.broadcasted_iota(jnp.int32, (4, 16, 512), 1)
    row = row + (zl * 128 + y * 32)
    col = lax.broadcasted_iota(jnp.int32, (4, 16, 512), 2)
    part = lax.broadcasted_iota(jnp.int32, (4, 16, 512), 0) // 2
    edge = jnp.maximum(row, col)

    def mask_wave(k, carry):
        cc, xx = k // 4, k % 4
        size = jnp.where(part == 0, sizes[2 * k], sizes[2 * k + 1])
        va[zl, cc, xx] = jnp.where(edge < size, wbuf[cc, xx].astype(F32), 0.0).astype(BF)
        return carry

    lax.fori_loop(0, 8, mask_wave, 0)
    pl.semaphore_wait(barrier, len(partners))
    for d in (2, -2):
        pl.semaphore_signal(relay.at[0], inc=1, device_id=to_z(d), device_id_type=MESH)

    z_of = [zl, (zl + 3) % 4, (zl + 1) % 4, (zl + 2) % 4]


    def gather(v, whole_slab):
        a1, b1, a2, b2, cx = copies(4), copies(3), copies(12), copies(16), copies(4)
        mine = v.at[zl, c, x]
        low = mine.at[pl.ds(0, 2)]
        send(low, low, a1, to_z(1))
        send(low, low, a1 + 1, to_z(-1))
        send(mine.at[0], mine.at[0], a1 + 2, to_z(2))
        send(mine.at[1], mine.at[1], a1 + 3, to_z(-2))

        def b2_send(xx, k):
            high = v.at[zl, c, xx, pl.ds(2, 2)]
            send(high, high, b2 + 4 * k, to_z(1))
            send(high, high, b2 + 4 * k + 1, to_z(-1))
            send(v.at[zl, c, xx, 2], v.at[zl, c, xx, 2], b2 + 4 * k + 2, to_z(2))
            send(v.at[zl, c, xx, 3], v.at[zl, c, xx, 3], b2 + 4 * k + 3, to_z(-2))

        def a2_send(k):
            block = v.at[z_of[k], c, x, pl.ds(0, 2)]
            for d in (1, 2, 3):
                send(block, block, a2 + 3 * k + d - 1, to_x(d))

        def a1_wait(k):
            block = v.at[z_of[k], c, x]
            if k < 3:
                arrived(block.at[pl.ds(0, 2)], a1 + k - 1)
            else:
                arrived(block.at[0], a1 + 2)
                arrived(block.at[1], a1 + 3)

        x_of = [x, (x + 3) % 4, (x + 1) % 4, (x + 2) % 4]
        step = [0, 1, 3, 2]
        if whole_slab:
            for k in range(4):
                b2_send(x_of[k], k)
        else:
            high = mine.at[pl.ds(2, 2)]
            for d in (1, 2, 3):
                send(high, high, b1 + d - 1, to_x(d))
            a2_send(0)
            b2_send(x, 0)
        for k in (1, 2, 3):
            if not whole_slab:
                arrived(v.at[zl, c, x_of[k], pl.ds(2, 2)], b1 + step[k] - 1)
                b2_send(x_of[k], k)
            a1_wait(k)
            a2_send(k)
        for k in range(4):
            if k == 0 and whole_slab:
                continue
            for m in (1, 2, 3):
                arrived(v.at[z_of[k], c, x_of[m], pl.ds(0, 2)], a2 + 3 * k + step[m] - 1)
            if k > 0:
                for m in range(4):
                    block = v.at[z_of[k], c, x_of[m]]
                    if k < 3:
                        arrived(block.at[pl.ds(2, 2)], b2 + 4 * m + k - 1)
                    else:
                        arrived(block.at[2], b2 + 4 * m + 2)
                        arrived(block.at[3], b2 + 4 * m + 3)
            send(v.at[z_of[k], c], v.at[z_of[k], c], cx + k, other)

        def other_core():
            for k in range(4):
                if k == 0 and whole_slab:
                    continue
                arrived(v.at[z_of[k], 1 - c], cx + k)

        return other_core

    def reduce(pair, tr, tc, s0s, s0r, s0, r1y, r1x, t1, t2, r2x, r2y, wf, wb, r3):
        p0, py, px, qx, qy, p3 = copies(4), copies(12), copies(3), copies(3), copies(3), copies(3)
        for k, d in enumerate((1, 2, 3, 0)):
            xx = (x + d) % 4
            s0s[xx] = pair(1 - c, xx).astype(BF)
            send(s0s.at[xx], s0r.at[xx], p0 + k, other)
        for k, d in enumerate((1, 2, 3, 0)):
            xx = (x + d) % 4
            total = pair(c, xx)
            arrived(s0r.at[xx], p0 + k)
            s0[xx] = (total + s0r[xx].astype(F32)).astype(BF)
            if d:
                send(s0.at[xx, 1], r1x.at[d - 1], px + d - 1, to_x(d))
            for e in (1, 2, 3):
                send(s0.at[xx, 0, (y + e) % 4], r1y.at[e - 1, xx], py + 3 * k + e - 1, to_y(e))


        def sum_t1(k, xx):
            total = s0[xx, 0, y].astype(F32)
            for e in (1, 2, 3):
                arrived(r1y.at[e - 1, xx], py + 3 * k + e - 1)
                total = total + r1y[e - 1, xx].astype(F32)
            return total

        def sum_t2(q):
            total = s0[x, 1, q].astype(F32)
            for d in (1, 2, 3):
                total = total + r1x[d - 1, q].astype(F32)
            return total

        for k, d in enumerate((1, 2, 3)):
            xx = (x + d) % 4
            t1[xx] = sum_t1(k, xx).astype(BF)
            send(t1.at[xx], r2x.at[d - 1], qx + d - 1, to_x(d))
        for d in (1, 2, 3):
            arrived(r1x.at[d - 1], px + d - 1)
        for e in (1, 2, 3):
            q = (y + e) % 4
            t2[q] = sum_t2(q).astype(BF)
            send(t2.at[q], r2y.at[e - 1], qy + e - 1, to_y(e))
        w0 = sum_t1(3, x)
        w1 = sum_t2(y)
        for d in (1, 2, 3):
            arrived(r2x.at[d - 1], qx + d - 1)
            w0 = w0 + r2x[d - 1].astype(F32)
        for d in (1, 2, 3):
            arrived(r2y.at[d - 1], qy + d - 1)
            w1 = w1 + r2y[d - 1].astype(F32)
        if tr == 32:
            pl.semaphore_wait(relay.at[1], 2)
        half = tr // 2
        for h, part_sum in enumerate((w0[:half], w0[half:], w1[:half], w1[half:])):
            wf[h] = part_sum
            wb[h] = part_sum.astype(BF)
        for d in (1, 2, 3):
            send(wb.at[(zh + d) % 4], r3.at[d - 1], p3 + d - 1, to_z(4 * d))
        total = wf[zh]
        for d in (1, 2, 3):
            arrived(r3.at[d - 1], p3 + d - 1)
            total = total + r3[d - 1].astype(F32)
        return total

    def pick(shape, kdim):
        k = lax.broadcasted_iota(jnp.int32, shape, kdim)
        m = lax.broadcasted_iota(jnp.int32, shape, 1 - kdim)
        return jnp.where(k == m // 32 * 128 + y * 32 + m % 32, 1.0, 0.0).astype(BF)

    other_core = gather(va, True)
    load_r.wait()
    load_l.wait()
    pick_t = pick((128, 512), 1)
    for t in range(3):
        rsel[pl.ds(128 * t, 128)] = dot(pick_t, rf[t], NT).astype(BF)
    pick_n = pick((512, 128), 0)
    for t in range(3):
        chosen = dot(lf[t], pick_n, NN).astype(BF)
        for zz in range(4):
            for q in range(4):
                for rh in range(2):
                    a = zz * 128 + q * 32 + rh * 16
                    b = q * 128 + rh * 64 + zz * 16
                    lsel[b : b + 16, 128 * t : 128 * t + 128] = chosen[a : a + 16]

    def left_half(cc):
        lrows = jnp.concatenate([lf[t, pl.ds(zl * 128, 128)] for t in range(3)], axis=0)

        def body(xx, carry):
            src = [va[:, cc, xx, pl.ds(2 * bp, 2)].reshape(128, 512) for bp in range(2)]
            res = dot(lrows, jnp.concatenate(src, axis=0), NT).astype(BF)
            for t in range(3):
                for bp in range(2):
                    mid[t, cc * 8 + xx * 2 + bp] = res[128 * t : 128 * t + 128, 128 * bp : 128 * bp + 128]
            return carry

        lax.fori_loop(0, 4, body, 0)

    left_half(c)
    other_core()
    left_half(1 - c)
    pl.semaphore_wait(relay.at[0], 2)
    for d in (4, -4):
        pl.semaphore_signal(relay.at[1], inc=1, device_id=to_z(d), device_id_type=MESH)

    def pair1(cc, xx):
        rows = []
        for bp in range(2):
            b = cc * 8 + xx * 2 + bp
            rows.append(jnp.concatenate([mid[t, pat[t, b]] for t in range(3)], axis=1))
        res = dot(jnp.concatenate(rows, axis=0), rsel[...], NN)
        return res.reshape(2, 4, 32, 512)

    total = reduce(pair1, 32, 512, s0s1, s0r1, s01, r1y1, r1x1, t11, t21, r2x1, r2y1, wf1, wb1, r31)
    b_mine = c * 8 + x * 2 + zh // 2
    size = sizes[b_mine]
    rr = lax.broadcasted_iota(jnp.int32, (16, 512), 0) + (zl * 128 + y * 32 + zh % 2 * 16)
    cc_ = lax.broadcasted_iota(jnp.int32, (16, 512), 1)
    piece = jnp.where(jnp.maximum(rr, cc_) < size, total, 0.0).astype(BF)
    f1[...] = piece
    g1 = copies(3)
    for d in (1, 2, 3):
        send(f1, vb.at[zl, c, x, zh], g1 + d - 1, to_z(4 * d))
    vb[zl, c, x, zh] = piece
    for d in (1, 2, 3):
        arrived(vb.at[zl, c, x, (zh + 4 - d) % 4], g1 + d - 1)

    other_core = gather(vb, False)

    def right_half(cc):
        rrows = jnp.concatenate([rf[t, pl.ds(zl * 128, 128)] for t in range(3)], axis=0)

        def body(xx, carry):
            src = [vb[:, cc, xx, pl.ds(2 * bp, 2)].reshape(128, 512) for bp in range(2)]
            res = dot(jnp.concatenate(src, axis=0), rrows, NT).astype(BF)
            for t in range(3):
                for bp in range(2):
                    mid[t, cc * 8 + xx * 2 + bp] = res[128 * bp : 128 * bp + 128, 128 * t : 128 * t + 128]
            return carry

        lax.fori_loop(0, 4, body, 0)

    right_half(c)
    other_core()
    store1 = pltpu.make_async_copy(vb.at[zl], out1, lsem.at[3])
    store1.start()
    right_half(1 - c)

    def pair2(cc, xx):
        cols = []
        for bp in range(2):
            b = cc * 8 + xx * 2 + bp
            cols.append(jnp.concatenate([mid[t, pat[t, b]] for t in range(3)], axis=0))
        res = dot(lsel[...], jnp.concatenate(cols, axis=1), NN)
        return jnp.stack([res[:, :128].reshape(4, 128, 128), res[:, 128:].reshape(4, 128, 128)])

    total = reduce(pair2, 128, 128, s0s2, s0r2, s02, r1y2, r1x2, t12, t22, r2x2, r2y2, wf2, wb2, r32)
    total = total.reshape(4, 16, 128)
    rr = lax.broadcasted_iota(jnp.int32, (4, 16, 128), 0) * 128 + lax.broadcasted_iota(jnp.int32, (4, 16, 128), 1)
    rr = rr + (y * 32 + zh % 2 * 16)
    cc_ = lax.broadcasted_iota(jnp.int32, (4, 16, 128), 2) + zl * 128
    piece = jnp.where(jnp.maximum(rr, cc_) < size, total, 0.0).astype(BF)
    f2[...] = piece
    g2 = copies(16)
    here = obuf.at[c, x, zh, :, pl.ds(pl.multiple_of(zl * 128, 128), 128)]
    own = pltpu.make_async_copy(f2.at[zl], here, lsem.at[4])
    own.start()
    for dl in range(4):
        for dh in range(4):
            if dl or dh:
                send(f2.at[(zl + dl) % 4], here, g2 + 4 * dl + dh, to_zz(dh, dl))
    own.wait()
    for dl in range(4):
        for dh in range(4):
            if dl or dh:
                zz = (zl + 4 - dl) % 4
                there = obuf.at[c, x, (zh + 4 - dh) % 4, :, pl.ds(pl.multiple_of(zz * 128, 128), 128)]
                arrived(there, g2 + 4 * dl + dh)
    gx, gc = copies(3), copies(4)
    for d in (1, 2, 3):
        send(obuf.at[c, x], obuf.at[c, x], gx + d - 1, to_x(d))
    send(obuf.at[c, x], obuf.at[c, x], gc, other)
    for d in (1, 3, 2):
        xx = (x + 4 - d) % 4
        arrived(obuf.at[c, xx], gx + d - 1)
        send(obuf.at[c, xx], obuf.at[c, xx], gc + d, other)
    for d in range(4):
        arrived(obuf.at[1 - c, (x + 4 - d) % 4], gc + d)
    store2 = pltpu.make_async_copy(obuf, out2, lsem.at[5])
    store2.start()
    store1.wait()
    store2.wait()
    for cp in sent:
        cp.wait_send()


N_COPIES = 39 + 28 + 3 + 39 + 28 + 16 + 7


def on_device(wave_t, left_ops, right_ops, pattern, sector_size):
    def stage(tr, tc):
        return [
            pltpu.VMEM((4, 2, 4, tr, tc), BF),
            pltpu.VMEM((4, 2, 4, tr, tc), BF),
            pltpu.VMEM((4, 2, 4, tr, tc), BF),
            pltpu.VMEM((3, 4, tr, tc), BF),
            pltpu.VMEM((3, 4, tr, tc), BF),
            pltpu.VMEM((4, tr, tc), BF),
            pltpu.VMEM((4, tr, tc), BF),
            pltpu.VMEM((3, tr, tc), BF),
            pltpu.VMEM((3, tr, tc), BF),
            pltpu.VMEM((4, tr // 2, tc), F32),
            pltpu.VMEM((4, tr // 2, tc), BF),
            pltpu.VMEM((3, tr // 2, tc), BF),
        ]

    hbm = pl.BlockSpec(memory_space=pl.ANY)
    fixed = pl.BlockSpec(memory_space=pltpu.HBM)
    smem = pl.BlockSpec(memory_space=pltpu.SMEM)
    out = jax.ShapeDtypeStruct((2, 4, 4, 16, 512), BF)
    first, second = pl.pallas_call(
        kernel,
        out_shape=(out, out),
        in_specs=[fixed, fixed, fixed, smem, smem],
        out_specs=(hbm, hbm),
        scratch_shapes=[
            pltpu.VMEM((2, 4, 4, 16, 512), BF),
            pltpu.VMEM((3, 512, 512), BF),
            pltpu.VMEM((3, 512, 512), BF),
            pltpu.VMEM((384, 512), BF),
            pltpu.VMEM((512, 384), BF),
            pltpu.VMEM((4, 2, 4, 4, 16, 512), BF),
            pltpu.VMEM((4, 2, 4, 4, 16, 512), BF),
            pltpu.VMEM((3, 16, 128, 128), BF),
            *stage(32, 512),
            pltpu.VMEM((16, 512), BF),
            *stage(128, 128),
            pltpu.VMEM((4, 16, 128), BF),
            pltpu.VMEM((2, 4, 4, 16, 512), BF),
            pltpu.SemaphoreType.DMA((6,)),
            pltpu.SemaphoreType.DMA((N_COPIES,)),
            pltpu.SemaphoreType.DMA((N_COPIES,)),
            pltpu.SemaphoreType.REGULAR((2,)),
        ],
        compiler_params=pltpu.CompilerParams(
            collective_id=0, has_side_effects=True, vmem_limit_bytes=48 * 2**20
        ),
        name="hamiltonian",
    )(wave_t.reshape(2, 4, 4, 16, 512), left_ops, right_ops, pattern, sector_size)
    return first.reshape(16, 32, 512), second.reshape(16, 32, 512)


def solution(mesh):
    return jax.shard_map(
        on_device,
        mesh=mesh,
        in_specs=(
            P(None, "sec", None),
            P("ops", None, None),
            P("ops", None, None),
            P("ops", None),
            P(),
        ),
        out_specs=(P(None, "sec", None), P(None, "sec", None)),
        check_vma=False,
    )
```

```python
import jax
import jax.numpy as jnp
from jax import lax
from jax.experimental import pallas as pl
from jax.experimental.pallas import tpu as pltpu
from jax.sharding import PartitionSpec as P

MESH = pl.DeviceIdType.MESH
BF = jnp.bfloat16
F32 = jnp.float32
NT = (((1,), (1,)), ((), ()))
NN = (((1,), (0,)), ((), ()))
N_STAGE = 13
N_COPIES = 500


def dot(a, b, dims):
    return lax.dot_general(a, b, dims, preferred_element_type=F32)


def kernel(wave, lops, rops, pat, sizes, out1, out2, *scratch):
    wbuf, lf, rf, rsel, lsel, va, vb, mid, f1, f2, obuf, lsem, ssem, rsem, relay = scratch[: -2 * N_STAGE]
    stage1, stage2 = scratch[-2 * N_STAGE : -N_STAGE], scratch[-N_STAGE:]
    ops, sec = lax.axis_index("ops"), lax.axis_index("sec")
    x, zh, c = ops // 8, (ops // 2) % 4, ops % 2
    zl, y = sec // 4, sec % 4
    z = zh * 4 + zl

    def to_x(d):
        return {"ops": ((x + d) % 4 * 4 + zh) * 2 + c, "sec": sec}

    def to_y(d):
        return {"ops": ops, "sec": zl * 4 + (y + d) % 4}

    def to_z(d):
        w = (z + d + 16) % 16
        return {"ops": (x * 4 + w // 4) * 2 + c, "sec": w % 4 * 4 + y}

    other = {"ops": ops + 1 - 2 * c, "sec": sec}

    sent = []
    relayed = [2]
    count = [0]

    def copies(n):
        first = count[0]
        count[0] += n
        return first

    def remote(src, dst, index, device, out_index=None):
        return pltpu.make_async_remote_copy(
            src_ref=src, dst_ref=dst, send_sem=ssem.at[index if out_index is None else out_index], recv_sem=rsem.at[index],
            device_id=device, device_id_type=MESH,
        )

    def send(src, dst, index, device, out_index=None):
        cp = remote(src, dst, index, device, out_index)
        cp.start()
        sent.append(cp)

    def arrived(ref, index):
        pltpu.make_async_copy(ref, ref, rsem.at[index]).wait()

    load_w = pltpu.make_async_copy(wave, wbuf, lsem.at[0])
    load_r = pltpu.make_async_copy(rops, rf, lsem.at[1])
    load_l = pltpu.make_async_copy(lops, lf, lsem.at[2])
    load_w.start()
    load_r.start()
    load_l.start()
    partners = [other] + [to_y(d) for d in (1, 2, 3)] + [to_x(d) for d in (1, 2, 3)] + [to_z(d) for d in (1, 2, -2, -1)]
    barrier = pltpu.get_barrier_semaphore()
    for device in partners:
        pl.semaphore_signal(barrier, inc=1, device_id=device, device_id_type=MESH)

    load_w.wait()
    row = lax.broadcasted_iota(jnp.int32, (16, 512), 0) + (zl * 128 + y * 32)
    col = lax.broadcasted_iota(jnp.int32, (16, 512), 1)

    def mask_wave(k, carry):
        cc, xx = k // 4, k % 4
        for rh in range(2):
            edge = jnp.maximum(row + 16 * rh, col)
            for bp in range(2):
                block = wbuf[cc, xx, bp, rh].astype(F32)
                va[zl, cc, xx, rh, bp] = jnp.where(edge < sizes[2 * k + bp], block, 0.0).astype(BF)
        return carry

    lax.fori_loop(0, 8, mask_wave, 0)
    pl.semaphore_wait(barrier, len(partners))
    for d in (2, -2):
        pl.semaphore_signal(relay.at[0], inc=1, device_id=to_z(d), device_id_type=MESH)

    z_of = [zl, (zl + 3) % 4, (zl + 1) % 4, (zl + 2) % 4]
    x_of = [x, (x + 3) % 4, (x + 1) % 4, (x + 2) % 4]
    step = [0, 1, 3, 2]

    def gather(v, chunk, whole_slab):
        halves = (0, 1) if chunk is None else (chunk,)
        rows = pl.ds(halves[0], len(halves))
        a1, b1, a2, b2, cx = copies(4), copies(3), copies(12), copies(16), copies(4)

        def z_send(xx, bp, i0):
            block = v.at[zl, c, xx, rows, bp]
            send(block, block, i0, to_z(1))
            send(block, block, i0 + 1, to_z(-1))
            for rh in halves:
                block = v.at[zl, c, xx, rh, bp]
                send(block, block, i0 + 2 + rh, to_z(2 - 4 * rh))

        def z_arrived(xx, bp, k, i0):
            if k < 3:
                arrived(v.at[z_of[k], c, xx, rows, bp], i0 + k - 1)
            else:
                for rh in halves:
                    arrived(v.at[z_of[k], c, xx, rh, bp], i0 + 2 + rh)

        def x_send(zz, bp, i0):
            block = v.at[zz, c, x, rows, bp]
            for d in (1, 2, 3):
                send(block, block, i0 + d - 1, to_x(d))

        z_send(x, 0, a1)
        if whole_slab:
            for k in range(4):
                z_send(x_of[k], 1, b2 + 4 * k)
        else:
            x_send(zl, 1, b1)
            x_send(zl, 0, a2)
            z_send(x, 1, b2)
        yield
        for k in (1, 2, 3):
            if not whole_slab:
                arrived(v.at[zl, c, x_of[k], rows, 1], b1 + step[k] - 1)
                z_send(x_of[k], 1, b2 + 4 * k)
            z_arrived(x, 0, k, a1)
            x_send(z_of[k], 0, a2 + 3 * k)
        yield
        for k in range(4):
            if k == 0 and whole_slab:
                continue
            for m in (1, 2, 3):
                arrived(v.at[z_of[k], c, x_of[m], rows, 0], a2 + 3 * k + step[m] - 1)
            if k > 0:
                for m in range(4):
                    z_arrived(x_of[m], 1, k, b2 + 4 * m)
            block = v.at[z_of[k], c, :, rows]
            send(block, block, cx + k, other)
        yield
        for k in range(4):
            if k == 0 and whole_slab:
                continue
            arrived(v.at[z_of[k], 1 - c, :, rows], cx + k)
        yield

    def run(flows, steps):
        for _ in range(steps):
            for flow in flows:
                next(flow)

    def drain():
        while sent:
            sent.pop().wait_send()

    def reduce(pair, half, cut, finish, s0s, s0r, s0, r1y, r1x, t1, t2, t2b, r2x, r2y, wf, wb, r3):
        p0, py, px, qx, qy, p3 = copies(4), copies(12), copies(6), copies(6), copies(6), copies(6)
        for k, d in enumerate((1, 2, 3, 0)):
            s0s[k] = pair(1 - c, (x + d) % 4).astype(BF)
            send(s0s.at[k], s0r.at[k], p0 + k, other)

        def first_sends(k, ch):
            if k < 3:
                send(s0.at[k, ch, 1], r1x.at[ch, k], px + 3 * ch + k, to_x(k + 1))
            if k % 2:
                for e in (1, 2, 3):
                    q = (y + e) % 4
                    send(s0.at[pl.ds(k - 1, 2), ch, 0, q], r1y.at[ch, e - 1, pl.ds(k - 1, 2)],
                         py + 6 * ch + 3 * (k // 2) + e - 1, to_y(e))

        for k, d in enumerate((1, 2, 3, 0)):
            total = pair(c, (x + d) % 4)
            arrived(s0r.at[k], p0 + k)
            total = total + s0r[k].astype(F32)
            for ch in range(2):
                for bp in range(2):
                    s0[k, ch, bp] = total[bp, :, ch * half : (ch + 1) * half].astype(BF)
            first_sends(k, 0)
        for k in range(4):
            first_sends(k, 1)

        def flow(ch):
            def sum_t1(k):
                total = s0[k, ch, 0, y].astype(F32)
                for e in (1, 2, 3):
                    total = total + r1y[ch, e - 1, k].astype(F32)
                return total

            for k in range(4):
                if k % 2 == 0:
                    for e in (1, 2, 3):
                        arrived(r1y.at[ch, e - 1, pl.ds(k, 2)], py + 6 * ch + 3 * (k // 2) + e - 1)
                if k < 3:
                    t1[ch, k] = sum_t1(k).astype(BF)
                    send(t1.at[ch, k], r2x.at[ch, k], qx + 3 * ch + k, to_x(k + 1))
            for k in range(3):
                arrived(r1x.at[ch, k], px + 3 * ch + k)
            mine = s0[3, ch, 1].astype(F32)
            for k in range(3):
                mine = mine + r1x[ch, k].astype(F32)
            t2[ch] = mine
            for e in (1, 2, 3):
                q = (y + e) % 4
                t2b[ch, e - 1] = t2[ch, q].astype(BF)
                send(t2b.at[ch, e - 1], r2y.at[ch, e - 1], qy + 3 * ch + e - 1, to_y(e))
            yield
            w0 = sum_t1(3)
            w1 = t2[ch, y]
            for k in range(3):
                arrived(r2x.at[ch, k], qx + 3 * ch + k)
                w0 = w0 + r2x[ch, k].astype(F32)
            for k in range(3):
                arrived(r2y.at[ch, k], qy + 3 * ch + k)
                w1 = w1 + r2y[ch, k].astype(F32)
            if relayed:
                pl.semaphore_wait(relay.at[1], relayed.pop())
            for bp, w in enumerate((w0, w1)):
                for part in range(2):
                    piece = cut(w, part)
                    wf[ch, 2 * bp + part] = piece
                    wb[ch, 2 * bp + part] = piece.astype(BF)
            for d in (1, 3, 2):
                send(wb.at[ch, (zh + d) % 4], r3.at[ch, d - 1], p3 + 3 * ch + d - 1, to_z(4 * d))
            yield
            total = wf[ch, zh]
            for d in (1, 3, 2):
                arrived(r3.at[ch, d - 1], p3 + 3 * ch + d - 1)
                total = total + r3[ch, d - 1].astype(F32)
            yield from finish(ch, total)

        return [flow(0), flow(1)]

    def pick(shape, kdim):
        k = lax.broadcasted_iota(jnp.int32, shape, kdim)
        m = lax.broadcasted_iota(jnp.int32, shape, 1 - kdim)
        return jnp.where(k == m // 32 * 128 + y * 32 + m % 32, 1.0, 0.0).astype(BF)

    start = gather(va, None, True)
    next(start)
    load_r.wait()
    load_l.wait()
    pick_t = pick((128, 512), 1)
    for t in range(3):
        rsel[pl.ds(128 * t, 128)] = dot(pick_t, rf[t], NT).astype(BF)
    next(start)
    next(start)

    def left_half(cc):
        lrows = jnp.concatenate([lf[t, pl.ds(zl * 128, 128)] for t in range(3)], axis=0)

        def body(xx, carry):
            src = [va[:, cc, xx, :, bp].reshape(128, 512) for bp in range(2)]
            res = dot(lrows, jnp.concatenate(src, axis=0), NT).astype(BF)
            for t in range(3):
                for bp in range(2):
                    mid[t, cc * 8 + xx * 2 + bp] = res[128 * t : 128 * t + 128, 128 * bp : 128 * bp + 128]
            return carry

        lax.fori_loop(0, 4, body, 0)

    left_half(c)
    next(start)
    left_half(1 - c)
    pl.semaphore_wait(relay.at[0], 2)
    for d in (4, -4):
        pl.semaphore_signal(relay.at[1], inc=1, device_id=to_z(d), device_id_type=MESH)

    def pair1(cc, xx):
        rows = []
        for bp in range(2):
            b = cc * 8 + xx * 2 + bp
            rows.append(jnp.concatenate([mid[t, pat[t, b]] for t in range(3)], axis=1))
        res = dot(jnp.concatenate(rows, axis=0), rsel[...], NN)
        return res.reshape(2, 4, 32, 512)

    b_mine = c * 8 + x * 2 + zh // 2

    def columns(part):
        return pl.ds(pl.multiple_of(part * 256, 256), 256)

    def finish1(ch, total):
        rr = lax.broadcasted_iota(jnp.int32, (16, 256), 0) + (zl * 128 + y * 32 + 16 * ch)
        cc_ = lax.broadcasted_iota(jnp.int32, (16, 256), 1) + zh % 2 * 256
        f1[ch] = jnp.where(jnp.maximum(rr, cc_) < sizes[b_mine], total, 0.0).astype(BF)
        here = vb.at[zl, c, x, ch, zh // 2, :, columns(zh % 2)]
        own = pltpu.make_async_copy(f1.at[ch], here, lsem.at[3 + ch])
        own.start()
        g1 = copies(3)
        for d in (1, 3, 2):
            send(f1.at[ch], here, g1 + d - 1, to_z(4 * d))
        yield
        own.wait()
        for d in (1, 3, 2):
            h = (zh + 4 - d) % 4
            arrived(vb.at[zl, c, x, ch, h // 2, :, columns(h % 2)], g1 + d - 1)
        yield from gather(vb, ch, False)

    flows = reduce(pair1, 16, lambda w, part: w[:, 256 * part : 256 * part + 256], finish1, *stage1)
    pick_n = pick((512, 128), 0)
    run(flows, 1)
    for t in range(3):
        chosen = dot(lf[t], pick_n, NN).astype(BF)
        for zz in range(4):
            for q in range(4):
                for rh in range(2):
                    a = zz * 128 + q * 32 + rh * 16
                    b = q * 128 + rh * 64 + zz * 16
                    lsel[b : b + 16, 128 * t : 128 * t + 128] = chosen[a : a + 16]
    run(flows, 5)

    def right_half(cc):
        rrows = jnp.concatenate([rf[t, pl.ds(zl * 128, 128)] for t in range(3)], axis=0)

        def body(xx, carry):
            src = [vb[:, cc, xx, :, bp].reshape(128, 512) for bp in range(2)]
            res = dot(jnp.concatenate(src, axis=0), rrows, NT).astype(BF)
            for t in range(3):
                for bp in range(2):
                    mid[t, cc * 8 + xx * 2 + bp] = res[128 * bp : 128 * bp + 128, 128 * t : 128 * t + 128]
            return carry

        lax.fori_loop(0, 4, body, 0)

    right_half(c)
    run(flows, 1)
    stores = []

    def store(src, dst, index):
        for rh in range(2):
            for bp in range(2):
                cp = pltpu.make_async_copy(src.at[:, :, rh, bp], dst.at[:, :, bp, rh], lsem.at[index + 2 * rh + bp])
                cp.start()
                stores.append(cp)

    store(vb.at[zl], out1, 5)
    right_half(1 - c)

    def pair2(cc, xx):
        cols = []
        for bp in range(2):
            b = cc * 8 + xx * 2 + bp
            cols.append(jnp.concatenate([mid[t, pat[t, b]] for t in range(3)], axis=0))
        res = dot(lsel[...], jnp.concatenate(cols, axis=1), NN)
        return jnp.stack([res[:, :128].reshape(4, 128, 128), res[:, 128:].reshape(4, 128, 128)])

    def finish2(ch, total):
        total = total.reshape(2, 16, 128)
        shape = (2, 16, 128)
        rr = lax.broadcasted_iota(jnp.int32, shape, 0) * 128 + lax.broadcasted_iota(jnp.int32, shape, 1)
        rr = rr + (zh % 2 * 256 + y * 32 + 16 * ch)
        cc_ = lax.broadcasted_iota(jnp.int32, shape, 2) + zl * 128
        f2[ch] = jnp.where(jnp.maximum(rr, cc_) < sizes[b_mine], total, 0.0).astype(BF)
        g2, out = copies(8), copies(8)
        here = obuf.at[c, x, ch, zh // 2, :, pl.ds(pl.multiple_of(zl * 128, 128), 128)]
        for i in range(2):
            to = zh % 2 * 2 + i
            for dh in (0, 1, 3, 2):
                device = {"ops": (x * 4 + (zh + dh) % 4) * 2 + c, "sec": to * 4 + y}
                if dh:
                    send(f2.at[ch, i], here, g2 + 4 * (dh // 2) + zl, device, out + 4 * i + dh)
                else:

                    @pl.when(to != zl)
                    def _():
                        remote(f2.at[ch, i], here, g2 + zl, device, out + 4 * i).start()

                    @pl.when(to == zl)
                    def _():
                        pltpu.make_async_copy(f2.at[ch, i], here, lsem.at[9 + ch]).start()

        yield
        for i in range(2):
            to = zh % 2 * 2 + i

            @pl.when(to != zl)
            def _():
                remote(f2.at[ch, i], here, g2 + zl, other, out + 4 * i).wait_send()

            @pl.when(to == zl)
            def _():
                pltpu.make_async_copy(f2.at[ch, i], here, lsem.at[9 + ch]).wait()

        odd = (zh + zl // 2) % 2
        for j in range(2):
            h = (zh + 4 - 2 * j - odd) % 4
            for zz in range(4):
                there = obuf.at[c, x, ch, h // 2, :, pl.ds(128 * zz, 128)]
                if j:
                    arrived(there, g2 + 4 + zz)
                else:

                    @pl.when((zz != zl) | (odd != 0))
                    def _():
                        arrived(there, g2 + zz)

        gx, gc = copies(3), copies(4)
        block = obuf.at[c, x, ch]
        for d in (1, 2, 3):
            send(block, block, gx + d - 1, to_x(d))
        send(block, block, gc, other)
        yield
        for d in (1, 3, 2):
            block = obuf.at[c, (x + 4 - d) % 4, ch]
            arrived(block, gx + d - 1)
            send(block, block, gc + d, other)
        yield
        for d in range(4):
            arrived(obuf.at[1 - c, (x + 4 - d) % 4, ch], gc + d)
        yield

    flows = reduce(pair2, 64, lambda w, part: w[32 * part : 32 * part + 32], finish2, *stage2)
    run(flows, 2)
    drain()
    run(flows, 4)
    store(obuf, out2, 11)
    drain()
    for cp in stores:
        cp.wait()
    assert count[0] <= N_COPIES, count


def on_device(wave_t, left_ops, right_ops, pattern, sector_size):
    def stage(r, w, piece):
        return [
            pltpu.VMEM((4, 2, 4, 2 * r, w), BF),
            pltpu.VMEM((4, 2, 4, 2 * r, w), BF),
            pltpu.VMEM((4, 2, 2, 4, r, w), BF),
            pltpu.VMEM((2, 3, 4, r, w), BF),
            pltpu.VMEM((2, 3, 4, r, w), BF),
            pltpu.VMEM((2, 3, r, w), BF),
            pltpu.VMEM((2, 4, r, w), F32),
            pltpu.VMEM((2, 3, r, w), BF),
            pltpu.VMEM((2, 3, r, w), BF),
            pltpu.VMEM((2, 3, r, w), BF),
            pltpu.VMEM((2, 4, *piece), F32),
            pltpu.VMEM((2, 4, *piece), BF),
            pltpu.VMEM((2, 3, *piece), BF),
        ]

    hbm = pl.BlockSpec(memory_space=pl.ANY)
    smem = pl.BlockSpec(memory_space=pltpu.SMEM)
    out = jax.ShapeDtypeStruct((2, 4, 2, 2, 16, 512), BF)
    first, second = pl.pallas_call(
        kernel,
        out_shape=(out, out),
        in_specs=[hbm, hbm, hbm, smem, smem],
        out_specs=(hbm, hbm),
        scratch_shapes=[
            pltpu.VMEM((2, 4, 2, 2, 16, 512), BF),
            pltpu.VMEM((3, 512, 512), BF),
            pltpu.VMEM((3, 512, 512), BF),
            pltpu.VMEM((384, 512), BF),
            pltpu.VMEM((512, 384), BF),
            pltpu.VMEM((4, 2, 4, 2, 2, 16, 512), BF),
            pltpu.VMEM((4, 2, 4, 2, 2, 16, 512), BF),
            pltpu.VMEM((3, 16, 128, 128), BF),
            pltpu.VMEM((2, 16, 256), BF),
            pltpu.VMEM((2, 2, 16, 128), BF),
            pltpu.VMEM((2, 4, 2, 2, 16, 512), BF),
            pltpu.SemaphoreType.DMA((16,)),
            pltpu.SemaphoreType.DMA((N_COPIES,)),
            pltpu.SemaphoreType.DMA((N_COPIES,)),
            pltpu.SemaphoreType.REGULAR((2,)),
            *stage(16, 512, (16, 256)),
            *stage(64, 128, (32, 128)),
        ],
        compiler_params=pltpu.CompilerParams(
            collective_id=0, has_side_effects=True, vmem_limit_bytes=58 * 2**20
        ),
        name="hamiltonian",
    )(wave_t.reshape(2, 4, 2, 2, 16, 512), left_ops, right_ops, pattern, sector_size)
    return first.reshape(16, 32, 512), second.reshape(16, 32, 512)


def solution(mesh):
    return jax.shard_map(
        on_device,
        mesh=mesh,
        in_specs=(
            P(None, "sec", None),
            P("ops", None, None),
            P("ops", None, None),
            P("ops", None),
            P(),
        ),
        out_specs=(P(None, "sec", None), P(None, "sec", None)),
        check_vma=False,
    )
```

```python
import jax
import jax.numpy as jnp
from jax import lax
from jax.experimental import pallas as pl
from jax.experimental.pallas import tpu as pltpu
from jax.sharding import PartitionSpec as P

MESH = pl.DeviceIdType.MESH
BF = jnp.bfloat16
F32 = jnp.float32
NT = (((1,), (1,)), ((), ()))
NN = (((1,), (0,)), ((), ()))
N_STAGE = 14
N_COPIES = 500


def dot(a, b, dims):
    return lax.dot_general(a, b, dims, preferred_element_type=F32)


def kernel(wave, lops, rops, pat, sizes, out1, out2, *scratch):
    wbuf, lf, rf, rsel, lsel, va, vb, mid, f2, obuf, lsem, ssem, rsem, relay = scratch[: -2 * N_STAGE]
    stage1, stage2 = scratch[-2 * N_STAGE : -N_STAGE], scratch[-N_STAGE:]
    ops, sec = lax.axis_index("ops"), lax.axis_index("sec")
    x, zh, c = ops // 8, (ops // 2) % 4, ops % 2
    zl, y = sec // 4, sec % 4
    z = zh * 4 + zl

    def to_x(d):
        return {"ops": ((x + d) % 4 * 4 + zh) * 2 + c, "sec": sec}

    def to_y(d):
        return {"ops": ops, "sec": zl * 4 + (y + d) % 4}

    def to_z(d):
        w = (z + d + 16) % 16
        return {"ops": (x * 4 + w // 4) * 2 + c, "sec": w % 4 * 4 + y}

    other = {"ops": ops + 1 - 2 * c, "sec": sec}

    sent = []
    count = [0]

    def copies(n):
        first = count[0]
        count[0] += n
        return first

    def remote(src, dst, index, device, out_index=None):
        return pltpu.make_async_remote_copy(
            src_ref=src, dst_ref=dst, send_sem=ssem.at[index if out_index is None else out_index], recv_sem=rsem.at[index],
            device_id=device, device_id_type=MESH,
        )

    def send(src, dst, index, device, out_index=None):
        cp = remote(src, dst, index, device, out_index)
        cp.start()
        sent.append(cp)

    def arrived(ref, index):
        pltpu.make_async_copy(ref, ref, rsem.at[index]).wait()

    load_w = pltpu.make_async_copy(wave, wbuf, lsem.at[0])
    load_r = pltpu.make_async_copy(rops, rf, lsem.at[1])
    load_l = pltpu.make_async_copy(lops, lf, lsem.at[2])
    load_w.start()
    load_r.start()
    load_l.start()
    partners = [other] + [to_y(d) for d in (1, 2, 3)] + [to_x(d) for d in (1, 2, 3)] + [to_z(d) for d in (1, 2, -2, -1)]
    barrier = pltpu.get_barrier_semaphore()
    for device in partners:
        pl.semaphore_signal(barrier, inc=1, device_id=device, device_id_type=MESH)

    load_w.wait()
    row = lax.broadcasted_iota(jnp.int32, (16, 512), 0) + (zl * 128 + y * 32)
    col = lax.broadcasted_iota(jnp.int32, (16, 512), 1)

    def mask_wave(k, carry):
        cc, xx = k // 4, k % 4
        for rh in range(2):
            edge = jnp.maximum(row + 16 * rh, col)
            for bp in range(2):
                block = wbuf[cc, xx, bp, rh].astype(F32)
                va[zl, cc, xx, rh, bp] = jnp.where(edge < sizes[2 * k + bp], block, 0.0).astype(BF)
        return carry

    lax.fori_loop(0, 8, mask_wave, 0)
    pl.semaphore_wait(barrier, len(partners))
    for d in (2, -2):
        pl.semaphore_signal(relay.at[0], inc=1, device_id=to_z(d), device_id_type=MESH)

    z_of = [zl, (zl + 3) % 4, (zl + 1) % 4, (zl + 2) % 4]
    x_of = [x, (x + 3) % 4, (x + 1) % 4, (x + 2) % 4]
    step = [0, 1, 3, 2]

    def gather(v, chunk, whole_slab):
        halves = (0, 1) if chunk is None else (chunk,)
        rows = pl.ds(halves[0], len(halves))
        a1, b1, a2, b2, cx = copies(4), copies(3), copies(12), copies(16), copies(4)

        def z_send(xx, bp, i0):
            block = v.at[zl, c, xx, rows, bp]
            send(block, block, i0, to_z(1))
            send(block, block, i0 + 1, to_z(-1))
            for rh in halves:
                block = v.at[zl, c, xx, rh, bp]
                send(block, block, i0 + 2 + rh, to_z(2 - 4 * rh))

        def z_arrived(xx, bp, k, i0):
            if k < 3:
                arrived(v.at[z_of[k], c, xx, rows, bp], i0 + k - 1)
            else:
                for rh in halves:
                    arrived(v.at[z_of[k], c, xx, rh, bp], i0 + 2 + rh)

        def x_send(zz, bp, i0):
            block = v.at[zz, c, x, rows, bp]
            for d in (1, 2, 3):
                send(block, block, i0 + d - 1, to_x(d))

        z_send(x, 0, a1)
        if whole_slab:
            for k in range(4):
                z_send(x_of[k], 1, b2 + 4 * k)
        else:
            x_send(zl, 1, b1)
            x_send(zl, 0, a2)
            z_send(x, 1, b2)
        yield
        for k in (1, 2, 3):
            if not whole_slab:
                arrived(v.at[zl, c, x_of[k], rows, 1], b1 + step[k] - 1)
                z_send(x_of[k], 1, b2 + 4 * k)
            z_arrived(x, 0, k, a1)
            x_send(z_of[k], 0, a2 + 3 * k)
        yield
        for k in range(4):
            if k == 0 and whole_slab:
                continue
            for m in (1, 2, 3):
                arrived(v.at[z_of[k], c, x_of[m], rows, 0], a2 + 3 * k + step[m] - 1)
            if k > 0:
                for m in range(4):
                    z_arrived(x_of[m], 1, k, b2 + 4 * m)
            block = v.at[z_of[k], c, :, rows]
            send(block, block, cx + k, other)
        yield
        for k in range(4):
            if k == 0 and whole_slab:
                continue
            arrived(v.at[z_of[k], 1 - c, :, rows], cx + k)
        yield

    def run(flows, steps):
        for _ in range(steps):
            for flow in flows:
                next(flow)

    def drain():
        while sent:
            sent.pop().wait_send()

    def reduce(pair, half, finish, s0s, s0r, s0, r1y, r1x, t1, t2, t2b, r2x, r2y, wb, z1, sb, z2):
        pair_z = 4 - 8 * (zh % 2)
        p0, py, px, qx, qy, p3 = copies(4), copies(12), copies(6), copies(6), copies(6), copies(8)
        def theirs(k):
            s0s[k] = pair(1 - c, (x + k + 1) % 4).astype(BF)
            send(s0s.at[k], s0r.at[k], p0 + k, other)

        def first_sends(k, ch):
            if k < 3:
                send(s0.at[k, ch, 1], r1x.at[ch, k], px + 3 * ch + k, to_x(k + 1))
            if k % 2:
                for e in (1, 2, 3):
                    q = (y + e) % 4
                    send(s0.at[pl.ds(k - 1, 2), ch, 0, q], r1y.at[ch, e - 1, pl.ds(k - 1, 2)],
                         py + 6 * ch + 3 * (k // 2) + e - 1, to_y(e))

        def ours(k):
            total = pair(c, (x + k + 1) % 4)
            arrived(s0r.at[k], p0 + k)
            total = total + s0r[k].astype(F32)
            for ch in range(2):
                for bp in range(2):
                    s0[k, ch, bp] = total[bp, :, ch * half : (ch + 1) * half].astype(BF)
            first_sends(k, 0)

        for k in (0, 1, 2):
            theirs(k)
        ours(0)
        theirs(3)
        for k in (1, 2, 3):
            ours(k)
        for k in range(4):
            first_sends(k, 1)

        def flow(ch):
            def sum_t1(k):
                total = s0[k, ch, 0, y].astype(F32)
                for e in (1, 2, 3):
                    total = total + r1y[ch, e - 1, k].astype(F32)
                return total

            for k in range(4):
                if k % 2 == 0:
                    for e in (1, 2, 3):
                        arrived(r1y.at[ch, e - 1, pl.ds(k, 2)], py + 6 * ch + 3 * (k // 2) + e - 1)
                if k < 3:
                    t1[ch, k] = sum_t1(k).astype(BF)
                    send(t1.at[ch, k], r2x.at[ch, k], qx + 3 * ch + k, to_x(k + 1))
            for k in range(3):
                arrived(r1x.at[ch, k], px + 3 * ch + k)
            mine = s0[3, ch, 1].astype(F32)
            for k in range(3):
                mine = mine + r1x[ch, k].astype(F32)
            t2[ch] = mine
            for e in (1, 2, 3):
                q = (y + e) % 4
                t2b[ch, e - 1] = t2[ch, q].astype(BF)
                send(t2b.at[ch, e - 1], r2y.at[ch, e - 1], qy + 3 * ch + e - 1, to_y(e))
            yield
            w0 = sum_t1(3)
            for k in range(3):
                arrived(r2x.at[ch, k], qx + 3 * ch + k)
                w0 = w0 + r2x[ch, k].astype(F32)
            wb[ch, 0] = w0.astype(BF)
            send(wb.at[ch, 0], z1.at[ch, 0], p3 + 4 * ch, to_z(pair_z))
            w1 = t2[ch, y]
            for k in range(3):
                arrived(r2y.at[ch, k], qy + 3 * ch + k)
                w1 = w1 + r2y[ch, k].astype(F32)
            wb[ch, 1] = w1.astype(BF)
            send(wb.at[ch, 1], z1.at[ch, 1], p3 + 4 * ch + 1, to_z(-pair_z))
            yield
            for bp, d in ((0, -pair_z), (1, pair_z)):
                arrived(z1.at[ch, bp], p3 + 4 * ch + bp)
                sb[ch, bp] = (wb[ch, bp].astype(F32) + z1[ch, bp].astype(F32)).astype(BF)
                send(sb.at[ch, bp], z2.at[ch, bp], p3 + 4 * ch + 2 + bp, to_z(d))
            yield
            for bp in range(2):
                arrived(z2.at[ch, bp], p3 + 4 * ch + 2 + bp)
            yield from finish(ch, [sb[ch, bp].astype(F32) + z2[ch, bp].astype(F32) for bp in range(2)])

        return [flow(0), flow(1)]

    def pick(shape, kdim):
        k = lax.broadcasted_iota(jnp.int32, shape, kdim)
        m = lax.broadcasted_iota(jnp.int32, shape, 1 - kdim)
        return jnp.where(k == m // 32 * 128 + y * 32 + m % 32, 1.0, 0.0).astype(BF)

    start = gather(va, None, True)
    next(start)
    next(start)
    load_r.wait()
    load_l.wait()
    pick_t = pick((128, 512), 1)
    for t in range(3):
        rsel[pl.ds(128 * t, 128)] = dot(pick_t, rf[t], NT).astype(BF)
    next(start)

    def left_half(cc):
        lrows = jnp.concatenate([lf[t, pl.ds(zl * 128, 128)] for t in range(3)], axis=0)

        def body(xx, carry):
            src = [va[:, cc, xx, :, bp].reshape(128, 512) for bp in range(2)]
            res = dot(lrows, jnp.concatenate(src, axis=0), NT).astype(BF)
            for t in range(3):
                for bp in range(2):
                    mid[t, cc * 8 + xx * 2 + bp] = res[128 * t : 128 * t + 128, 128 * bp : 128 * bp + 128]
            return carry

        lax.fori_loop(0, 4, body, 0)

    left_half(c)
    next(start)
    left_half(1 - c)
    pl.semaphore_wait(relay.at[0], 2)

    def pair1(cc, xx):
        rows = []
        for bp in range(2):
            b = cc * 8 + xx * 2 + bp
            rows.append(jnp.concatenate([mid[t, pat[t, b]] for t in range(3)], axis=1))
        res = dot(jnp.concatenate(rows, axis=0), rsel[...], NN)
        return res.reshape(2, 4, 32, 512)

    def finish1(ch, totals):
        rr = lax.broadcasted_iota(jnp.int32, (16, 512), 0) + (zl * 128 + y * 32 + 16 * ch)
        edge = jnp.maximum(rr, lax.broadcasted_iota(jnp.int32, (16, 512), 1))
        for bp in range(2):
            vb[zl, c, x, ch, bp] = jnp.where(edge < sizes[c * 8 + x * 2 + bp], totals[bp], 0.0).astype(BF)
        yield from gather(vb, ch, False)

    flows = reduce(pair1, 16, finish1, *stage1)
    pick_n = pick((512, 128), 0)
    run(flows, 2)
    for t in range(3):
        chosen = dot(lf[t], pick_n, NN).astype(BF)
        for zz in range(4):
            for q in range(4):
                for rh in range(2):
                    a = zz * 128 + q * 32 + rh * 16
                    b = q * 128 + rh * 64 + zz * 16
                    lsel[b : b + 16, 128 * t : 128 * t + 128] = chosen[a : a + 16]
    run(flows, 4)

    def right_half(cc):
        rrows = jnp.concatenate([rf[t, pl.ds(zl * 128, 128)] for t in range(3)], axis=0)

        def body(xx, carry):
            src = [vb[:, cc, xx, :, bp].reshape(128, 512) for bp in range(2)]
            res = dot(jnp.concatenate(src, axis=0), rrows, NT).astype(BF)
            for t in range(3):
                for bp in range(2):
                    mid[t, cc * 8 + xx * 2 + bp] = res[128 * bp : 128 * bp + 128, 128 * t : 128 * t + 128]
            return carry

        lax.fori_loop(0, 4, body, 0)

    right_half(c)
    run(flows, 1)
    stores = []

    def store(src, dst, index):
        for rh in range(2):
            for bp in range(2):
                cp = pltpu.make_async_copy(src.at[:, :, rh, bp], dst.at[:, :, bp, rh], lsem.at[index + 2 * rh + bp])
                cp.start()
                stores.append(cp)

    store(vb.at[zl], out1, 5)
    right_half(1 - c)

    def pair2(cc, xx):
        cols = []
        for bp in range(2):
            b = cc * 8 + xx * 2 + bp
            cols.append(jnp.concatenate([mid[t, pat[t, b]] for t in range(3)], axis=0))
        res = dot(lsel[...], jnp.concatenate(cols, axis=1), NN)
        return jnp.stack([res[:, :128].reshape(4, 128, 128), res[:, 128:].reshape(4, 128, 128)])

    def lanes(zz):
        return pl.ds(pl.multiple_of(zz * 128, 128), 128)

    def finish2(ch, totals):
        shape = (4, 16, 128)
        rr = lax.broadcasted_iota(jnp.int32, shape, 0) * 128 + lax.broadcasted_iota(jnp.int32, shape, 1)
        edge = jnp.maximum(rr + (y * 32 + 16 * ch), lax.broadcasted_iota(jnp.int32, shape, 2) + zl * 128)
        for bp in range(2):
            f2[ch, bp] = jnp.where(edge < sizes[c * 8 + x * 2 + bp], totals[bp].reshape(shape), 0.0).astype(BF)
        here = obuf.at[c, x, ch, :, :, lanes(zl)]
        own = pltpu.make_async_copy(f2.at[ch, :, zl], here, lsem.at[3 + ch])
        own.start()
        g2 = copies(3)
        away = (1, -1, 2 - 4 * ch)
        for k, d in enumerate(away):
            send(f2.at[ch, :, (zl + d + 4) % 4], here, g2 + k, to_z(d))
        yield
        own.wait()
        for k, d in enumerate(away):
            arrived(obuf.at[c, x, ch, :, :, lanes((zl - d + 4) % 4)], g2 + k)
        gx, gc = copies(3), copies(4)
        block = obuf.at[c, x, ch]
        for d in (1, 2, 3):
            send(block, block, gx + d - 1, to_x(d))
        send(block, block, gc, other)
        yield
        for d in (1, 3, 2):
            block = obuf.at[c, (x + 4 - d) % 4, ch]
            arrived(block, gx + d - 1)
            send(block, block, gc + d, other)
        yield
        for d in range(4):
            arrived(obuf.at[1 - c, (x + 4 - d) % 4, ch], gc + d)
        yield

    flows = reduce(pair2, 64, finish2, *stage2)
    run(flows, 2)
    drain()
    run(flows, 5)
    store(obuf, out2, 11)
    drain()
    for cp in stores:
        cp.wait()
    assert count[0] <= N_COPIES, count


def on_device(wave_t, left_ops, right_ops, pattern, sector_size):
    def stage(r, w):
        return [
            pltpu.VMEM((4, 2, 4, 2 * r, w), BF),
            pltpu.VMEM((4, 2, 4, 2 * r, w), BF),
            pltpu.VMEM((4, 2, 2, 4, r, w), BF),
            pltpu.VMEM((2, 3, 4, r, w), BF),
            pltpu.VMEM((2, 3, 4, r, w), BF),
            pltpu.VMEM((2, 3, r, w), BF),
            pltpu.VMEM((2, 4, r, w), F32),
            pltpu.VMEM((2, 3, r, w), BF),
            pltpu.VMEM((2, 3, r, w), BF),
            pltpu.VMEM((2, 3, r, w), BF),
            pltpu.VMEM((2, 2, r, w), BF),
            pltpu.VMEM((2, 2, r, w), BF),
            pltpu.VMEM((2, 2, r, w), BF),
            pltpu.VMEM((2, 2, r, w), BF),
        ]

    hbm = pl.BlockSpec(memory_space=pl.ANY)
    smem = pl.BlockSpec(memory_space=pltpu.SMEM)
    out = jax.ShapeDtypeStruct((2, 4, 2, 2, 16, 512), BF)
    first, second = pl.pallas_call(
        kernel,
        out_shape=(out, out),
        in_specs=[hbm, hbm, hbm, smem, smem],
        out_specs=(hbm, hbm),
        scratch_shapes=[
            pltpu.VMEM((2, 4, 2, 2, 16, 512), BF),
            pltpu.VMEM((3, 512, 512), BF),
            pltpu.VMEM((3, 512, 512), BF),
            pltpu.VMEM((384, 512), BF),
            pltpu.VMEM((512, 384), BF),
            pltpu.VMEM((4, 2, 4, 2, 2, 16, 512), BF),
            pltpu.VMEM((4, 2, 4, 2, 2, 16, 512), BF),
            pltpu.VMEM((3, 16, 128, 128), BF),
            pltpu.VMEM((2, 2, 4, 16, 128), BF),
            pltpu.VMEM((2, 4, 2, 2, 16, 512), BF),
            pltpu.SemaphoreType.DMA((16,)),
            pltpu.SemaphoreType.DMA((N_COPIES,)),
            pltpu.SemaphoreType.DMA((N_COPIES,)),
            pltpu.SemaphoreType.REGULAR((1,)),
            *stage(16, 512),
            *stage(64, 128),
        ],
        compiler_params=pltpu.CompilerParams(
            collective_id=0, has_side_effects=True, vmem_limit_bytes=58 * 2**20
        ),
        name="hamiltonian",
    )(wave_t.reshape(2, 4, 2, 2, 16, 512), left_ops, right_ops, pattern, sector_size)
    return first.reshape(16, 32, 512), second.reshape(16, 32, 512)


def solution(mesh):
    return jax.shard_map(
        on_device,
        mesh=mesh,
        in_specs=(
            P(None, "sec", None),
            P("ops", None, None),
            P("ops", None, None),
            P("ops", None),
            P(),
        ),
        out_specs=(P(None, "sec", None), P(None, "sec", None)),
        check_vma=False,
    )
```

```python
import jax
import jax.numpy as jnp
from jax import lax
from jax.experimental import pallas as pl
from jax.experimental.pallas import tpu as pltpu
from jax.sharding import PartitionSpec as P

MESH = pl.DeviceIdType.MESH
BF = jnp.bfloat16
F32 = jnp.float32
NT = (((1,), (1,)), ((), ()))
NN = (((1,), (0,)), ((), ()))
N_STAGE = 14
N_ARRIVALS = 106
N_SENDS = 56


def dot(a, b, dims):
    return lax.dot_general(a, b, dims, preferred_element_type=F32)


def kernel(wave, lops, rops, pat, sizes, out1, out2, *scratch):
    wbuf, lf, rf, rsel, lsel, va, vb, mid, f2, obuf, lsem, ssem, rsem, relay = scratch[: -2 * N_STAGE]
    stage1, stage2 = scratch[-2 * N_STAGE : -N_STAGE], scratch[-N_STAGE:]
    ops, sec = lax.axis_index("ops"), lax.axis_index("sec")
    x, zh, c = ops // 8, (ops // 2) % 4, ops % 2
    zl, y = sec // 4, sec % 4
    z = zh * 4 + zl

    def to_x(d):
        return {"ops": ((x + d) % 4 * 4 + zh) * 2 + c, "sec": sec}

    def to_y(d):
        return {"ops": ops, "sec": zl * 4 + (y + d) % 4}

    def to_z(d):
        w = (z + d + 16) % 16
        return {"ops": (x * 4 + w // 4) * 2 + c, "sec": w % 4 * 4 + y}

    other = {"ops": ops + 1 - 2 * c, "sec": sec}

    sent = []
    count = [0]

    def copies(n):
        first = count[0]
        count[0] += n
        return first

    def send_all(group, total):
        i = len(sent)
        assert i < N_SENDS, i
        for src, dst, index, device in group:
            pltpu.make_async_remote_copy(
                src_ref=src, dst_ref=dst, send_sem=ssem.at[i], recv_sem=rsem.at[index],
                device_id=device, device_id_type=MESH,
            ).start()
        sent.append(pltpu.make_async_copy(total, total, ssem.at[i]))

    def send(src, dst, index, device):
        send_all([(src, dst, index, device)], src)

    def drain():
        while sent:
            sent.pop().wait()

    def arrived(ref, index):
        pltpu.make_async_copy(ref, ref, rsem.at[index]).wait()

    load_w = pltpu.make_async_copy(wave, wbuf, lsem.at[0])
    load_r = pltpu.make_async_copy(rops, rf, lsem.at[1])
    load_l = pltpu.make_async_copy(lops, lf, lsem.at[2])
    load_w.start()
    load_r.start()
    load_l.start()
    partners = [other] + [to_y(d) for d in (1, 2, 3)] + [to_x(d) for d in (1, 2, 3)] + [to_z(d) for d in (1, 2, -2, -1)]
    barrier = pltpu.get_barrier_semaphore()
    for device in partners:
        pl.semaphore_signal(barrier, inc=1, device_id=device, device_id_type=MESH)

    load_w.wait()
    row = lax.broadcasted_iota(jnp.int32, (16, 512), 0) + (zl * 128 + y * 32)
    col = lax.broadcasted_iota(jnp.int32, (16, 512), 1)

    def mask_wave(k, carry):
        cc, xx = k // 4, k % 4
        for rh in range(2):
            edge = jnp.maximum(row + 16 * rh, col)
            for bp in range(2):
                block = wbuf[cc, xx, bp, rh].astype(F32)
                va[zl, cc, xx, rh, bp] = jnp.where(edge < sizes[2 * k + bp], block, 0.0).astype(BF)
        return carry

    lax.fori_loop(0, 8, mask_wave, 0)
    pl.semaphore_wait(barrier, len(partners))
    for d in (2, -2):
        pl.semaphore_signal(relay.at[0], inc=1, device_id=to_z(d), device_id_type=MESH)

    z_of = [zl, (zl + 3) % 4, (zl + 1) % 4, (zl + 2) % 4]
    x_of = [x, (x + 3) % 4, (x + 1) % 4, (x + 2) % 4]
    step = [0, 1, 3, 2]

    def gather(v, chunk, whole_slab):
        halves = (0, 1) if chunk is None else (chunk,)
        rows = pl.ds(halves[0], len(halves))
        a1, b1, a2, b2, cx = copies(4), copies(3), copies(4), copies(4), copies(1)

        def z_send(xx, bp, i0):
            block = v.at[zl, c, xx, rows, bp]
            group = [(block, block, i0, to_z(1)), (block, block, i0 + 1, to_z(-1))]
            for rh in halves:
                part = v.at[zl, c, xx, rh, bp]
                group.append((part, part, i0 + 2 + rh, to_z(2 - 4 * rh)))
            send_all(group, v.at[zl, c, pl.ds(0, 3), rows, bp])

        def z_arrived(xx, bp, k, i0):
            if k < 3:
                arrived(v.at[z_of[k], c, xx, rows, bp], i0 + k - 1)
            else:
                for rh in halves:
                    arrived(v.at[z_of[k], c, xx, rh, bp], i0 + 2 + rh)

        def x_send(zz, bp, indices):
            block = v.at[zz, c, x, rows, bp]
            group = [(block, block, i, to_x(d)) for d, i in zip((1, 2, 3), indices)]
            send_all(group, v.at[zz, c, pl.ds(0, 3), rows, bp])

        z_send(x, 0, a1)
        if whole_slab:
            for k in range(4):
                z_send(x_of[k], 1, b2)
        else:
            x_send(zl, 1, (b1, b1 + 1, b1 + 2))
            x_send(zl, 0, (a2, a2, a2))
            z_send(x, 1, b2)
        yield
        for k in (1, 2, 3):
            if not whole_slab:
                arrived(v.at[zl, c, x_of[k], rows, 1], b1 + step[k] - 1)
                z_send(x_of[k], 1, b2)
            z_arrived(x, 0, k, a1)
            x_send(z_of[k], 0, (a2 + k, a2 + k, a2 + k))
        yield
        for k in range(4):
            if k == 0 and whole_slab:
                continue
            arrived(v.at[z_of[k], c, pl.ds(0, 3), rows, 0], a2 + k)
            if k > 0:
                z_arrived(slice(None), 1, k, b2)
            block = v.at[z_of[k], c, :, rows]
            send(block, block, cx, other)
        yield
        arrived(v.at[pl.ds(0, 3 if whole_slab else 4), 1 - c, :, rows], cx)
        yield

    def run(flows, steps):
        for _ in range(steps):
            for flow in flows:
                next(flow)

    def reduce(pair, half, finish, s0s, s0r, s0, r1y, r1x, t1, t2, t2b, r2x, r2y, wb, z1, sb, z2):
        pair_z = 4 - 8 * (zh % 2)
        p0, py, px, qx, qy, p3 = copies(4), copies(4), copies(2), copies(2), copies(2), copies(8)
        def theirs(k):
            s0s[k] = pair(1 - c, (x + k + 1) % 4).astype(BF)
            send(s0s.at[k], s0r.at[k], p0 + k, other)

        def first_sends(k, ch):
            if k < 3:
                send(s0.at[k, ch, 1], r1x.at[ch, k], px + ch, to_x(k + 1))
            if k % 2:
                two = pl.ds(k - 1, 2)
                group = [
                    (s0.at[two, ch, 0, (y + e) % 4], r1y.at[ch, e - 1, two], py + 2 * ch + k // 2, to_y(e)) for e in (1, 2, 3)
                ]
                send_all(group, r1y.at[ch, :, two])

        def ours(k):
            total = pair(c, (x + k + 1) % 4)
            arrived(s0r.at[k], p0 + k)
            total = total + s0r[k].astype(F32)
            for ch in range(2):
                for bp in range(2):
                    s0[k, ch, bp] = total[bp, :, ch * half : (ch + 1) * half].astype(BF)
            first_sends(k, 0)

        for k in (0, 1, 2):
            theirs(k)
        ours(0)
        theirs(3)
        for k in (1, 2, 3):
            ours(k)
        for k in range(4):
            first_sends(k, 1)

        def flow(ch):
            def sum_t1(k):
                total = s0[k, ch, 0, y].astype(F32)
                for e in (1, 2, 3):
                    total = total + r1y[ch, e - 1, k].astype(F32)
                return total

            for k in range(4):
                if k % 2 == 0:
                    arrived(r1y.at[ch, :, pl.ds(k, 2)], py + 2 * ch + k // 2)
                if k < 3:
                    t1[ch, k] = sum_t1(k).astype(BF)
                    if k == 2:
                        group = [(t1.at[ch, m], r2x.at[ch, m], qx + ch, to_x(m + 1)) for m in range(3)]
                        send_all(group, r2x.at[ch])
            arrived(r1x.at[ch], px + ch)
            mine = s0[3, ch, 1].astype(F32)
            for k in range(3):
                mine = mine + r1x[ch, k].astype(F32)
            t2[ch] = mine
            for e in (1, 2, 3):
                q = (y + e) % 4
                t2b[ch, e - 1] = t2[ch, q].astype(BF)
            group = [(t2b.at[ch, e - 1], r2y.at[ch, e - 1], qy + ch, to_y(e)) for e in (1, 2, 3)]
            send_all(group, r2y.at[ch])
            yield
            w0 = sum_t1(3)
            arrived(r2x.at[ch], qx + ch)
            for k in range(3):
                w0 = w0 + r2x[ch, k].astype(F32)
            wb[ch, 0] = w0.astype(BF)
            send(wb.at[ch, 0], z1.at[ch, 0], p3 + 4 * ch, to_z(pair_z))
            w1 = t2[ch, y]
            arrived(r2y.at[ch], qy + ch)
            for k in range(3):
                w1 = w1 + r2y[ch, k].astype(F32)
            wb[ch, 1] = w1.astype(BF)
            send(wb.at[ch, 1], z1.at[ch, 1], p3 + 4 * ch + 1, to_z(-pair_z))
            yield
            for bp, d in ((0, -pair_z), (1, pair_z)):
                arrived(z1.at[ch, bp], p3 + 4 * ch + bp)
                sb[ch, bp] = (wb[ch, bp].astype(F32) + z1[ch, bp].astype(F32)).astype(BF)
                send(sb.at[ch, bp], z2.at[ch, bp], p3 + 4 * ch + 2 + bp, to_z(d))
            yield
            for bp in range(2):
                arrived(z2.at[ch, bp], p3 + 4 * ch + 2 + bp)
            yield from finish(ch, [sb[ch, bp].astype(F32) + z2[ch, bp].astype(F32) for bp in range(2)])

        return [flow(0), flow(1)]

    def pick(shape, kdim):
        k = lax.broadcasted_iota(jnp.int32, shape, kdim)
        m = lax.broadcasted_iota(jnp.int32, shape, 1 - kdim)
        return jnp.where(k == m // 32 * 128 + y * 32 + m % 32, 1.0, 0.0).astype(BF)

    start = gather(va, None, True)
    next(start)
    next(start)
    load_r.wait()
    load_l.wait()
    pick_t = pick((128, 512), 1)
    for t in range(3):
        rsel[pl.ds(128 * t, 128)] = dot(pick_t, rf[t], NT).astype(BF)
    next(start)

    def left_half(cc):
        lrows = jnp.concatenate([lf[t, pl.ds(zl * 128, 128)] for t in range(3)], axis=0)

        def body(xx, carry):
            src = [va[:, cc, xx, :, bp].reshape(128, 512) for bp in range(2)]
            res = dot(lrows, jnp.concatenate(src, axis=0), NT).astype(BF)
            for t in range(3):
                for bp in range(2):
                    mid[t, cc * 8 + xx * 2 + bp] = res[128 * t : 128 * t + 128, 128 * bp : 128 * bp + 128]
            return carry

        lax.fori_loop(0, 4, body, 0)

    left_half(c)
    next(start)
    left_half(1 - c)
    pl.semaphore_wait(relay.at[0], 2)

    def pair1(cc, xx):
        rows = []
        for bp in range(2):
            b = cc * 8 + xx * 2 + bp
            rows.append(jnp.concatenate([mid[t, pat[t, b]] for t in range(3)], axis=1))
        res = dot(jnp.concatenate(rows, axis=0), rsel[...], NN)
        return res.reshape(2, 4, 32, 512)

    def finish1(ch, totals):
        rr = lax.broadcasted_iota(jnp.int32, (16, 512), 0) + (zl * 128 + y * 32 + 16 * ch)
        edge = jnp.maximum(rr, lax.broadcasted_iota(jnp.int32, (16, 512), 1))
        for bp in range(2):
            vb[zl, c, x, ch, bp] = jnp.where(edge < sizes[c * 8 + x * 2 + bp], totals[bp], 0.0).astype(BF)
        yield from gather(vb, ch, False)

    flows = reduce(pair1, 16, finish1, *stage1)
    pick_n = pick((512, 128), 0)
    run(flows, 2)
    drain()
    for t in range(3):
        chosen = dot(lf[t], pick_n, NN).astype(BF)
        for zz in range(4):
            for q in range(4):
                for rh in range(2):
                    a = zz * 128 + q * 32 + rh * 16
                    b = q * 128 + rh * 64 + zz * 16
                    lsel[b : b + 16, 128 * t : 128 * t + 128] = chosen[a : a + 16]
    run(flows, 4)

    def right_half(cc):
        rrows = jnp.concatenate([rf[t, pl.ds(zl * 128, 128)] for t in range(3)], axis=0)

        def body(xx, carry):
            src = [vb[:, cc, xx, :, bp].reshape(128, 512) for bp in range(2)]
            res = dot(jnp.concatenate(src, axis=0), rrows, NT).astype(BF)
            for t in range(3):
                for bp in range(2):
                    mid[t, cc * 8 + xx * 2 + bp] = res[128 * bp : 128 * bp + 128, 128 * t : 128 * t + 128]
            return carry

        lax.fori_loop(0, 4, body, 0)

    right_half(c)
    run(flows, 1)
    stores = []

    def store(src, dst, index):
        for rh in range(2):
            for bp in range(2):
                cp = pltpu.make_async_copy(src.at[:, :, rh, bp], dst.at[:, :, bp, rh], lsem.at[index + 2 * rh + bp])
                cp.start()
                stores.append(cp)

    store(vb.at[zl], out1, 5)
    right_half(1 - c)

    def pair2(cc, xx):
        cols = []
        for bp in range(2):
            b = cc * 8 + xx * 2 + bp
            cols.append(jnp.concatenate([mid[t, pat[t, b]] for t in range(3)], axis=0))
        res = dot(lsel[...], jnp.concatenate(cols, axis=1), NN)
        return jnp.stack([res[:, :128].reshape(4, 128, 128), res[:, 128:].reshape(4, 128, 128)])

    def lanes(zz):
        return pl.ds(pl.multiple_of(zz * 128, 128), 128)

    def finish2(ch, totals):
        shape = (4, 16, 128)
        rr = lax.broadcasted_iota(jnp.int32, shape, 0) * 128 + lax.broadcasted_iota(jnp.int32, shape, 1)
        edge = jnp.maximum(rr + (y * 32 + 16 * ch), lax.broadcasted_iota(jnp.int32, shape, 2) + zl * 128)
        for bp in range(2):
            f2[ch, bp] = jnp.where(edge < sizes[c * 8 + x * 2 + bp], totals[bp].reshape(shape), 0.0).astype(BF)
        here = obuf.at[c, x, ch, :, :, lanes(zl)]
        own = pltpu.make_async_copy(f2.at[ch, :, zl], here, lsem.at[3 + ch])
        own.start()
        g2 = copies(3)
        away = (1, -1, 2 - 4 * ch)
        for k, d in enumerate(away):
            send(f2.at[ch, :, (zl + d + 4) % 4], here, g2 + k, to_z(d))
        yield
        own.wait()
        for k, d in enumerate(away):
            arrived(obuf.at[c, x, ch, :, :, lanes((zl - d + 4) % 4)], g2 + k)
        gx, gc = copies(3), copies(1)
        block = obuf.at[c, x, ch]
        send_all([(block, block, gx + d - 1, to_x(d)) for d in (1, 2, 3)], obuf.at[c, pl.ds(0, 3), ch])
        send(block, block, gc, other)
        yield
        for d in (1, 3, 2):
            block = obuf.at[c, (x + 4 - d) % 4, ch]
            arrived(block, gx + d - 1)
            send(block, block, gc, other)
        yield
        arrived(obuf.at[1 - c, :, ch], gc)
        yield

    flows = reduce(pair2, 64, finish2, *stage2)
    run(flows, 2)
    drain()
    run(flows, 5)
    store(obuf, out2, 11)
    drain()
    for cp in stores:
        cp.wait()
    assert count[0] == N_ARRIVALS, count


def hand_over(first, second, out1, out2, sem):
    cps = []
    for i, (src, dst) in enumerate(((first, out1), (second, out2))):
        for cc in range(2):
            for part in range(2):
                where = (cc, pl.ds(2 * part, 2))
                cps.append(pltpu.make_async_copy(src.at[where], dst.at[where], sem.at[4 * i + 2 * cc + part]))
    for cp in cps:
        cp.start()
    for cp in cps:
        cp.wait()


def on_device(wave_t, left_ops, right_ops, pattern, sector_size):
    def stage(r, w):
        return [
            pltpu.VMEM((4, 2, 4, 2 * r, w), BF),
            pltpu.VMEM((4, 2, 4, 2 * r, w), BF),
            pltpu.VMEM((4, 2, 2, 4, r, w), BF),
            pltpu.VMEM((2, 3, 4, r, w), BF),
            pltpu.VMEM((2, 3, 4, r, w), BF),
            pltpu.VMEM((2, 3, r, w), BF),
            pltpu.VMEM((2, 4, r, w), F32),
            pltpu.VMEM((2, 3, r, w), BF),
            pltpu.VMEM((2, 3, r, w), BF),
            pltpu.VMEM((2, 3, r, w), BF),
            pltpu.VMEM((2, 2, r, w), BF),
            pltpu.VMEM((2, 2, r, w), BF),
            pltpu.VMEM((2, 2, r, w), BF),
            pltpu.VMEM((2, 2, r, w), BF),
        ]

    hbm = pl.BlockSpec(memory_space=pl.ANY)
    smem = pl.BlockSpec(memory_space=pltpu.SMEM)
    out = jax.ShapeDtypeStruct((2, 4, 2, 2, 16, 512), BF)
    first, second = pl.pallas_call(
        kernel,
        out_shape=(out, out),
        in_specs=[hbm, hbm, hbm, smem, smem],
        out_specs=(hbm, hbm),
        scratch_shapes=[
            pltpu.VMEM((2, 4, 2, 2, 16, 512), BF),
            pltpu.VMEM((3, 512, 512), BF),
            pltpu.VMEM((3, 512, 512), BF),
            pltpu.VMEM((384, 512), BF),
            pltpu.VMEM((512, 384), BF),
            pltpu.VMEM((4, 2, 4, 2, 2, 16, 512), BF),
            pltpu.VMEM((4, 2, 4, 2, 2, 16, 512), BF),
            pltpu.VMEM((3, 16, 128, 128), BF),
            pltpu.VMEM((2, 2, 4, 16, 128), BF),
            pltpu.VMEM((2, 4, 2, 2, 16, 512), BF),
            pltpu.SemaphoreType.DMA((16,)),
            pltpu.SemaphoreType.DMA((N_SENDS,)),
            pltpu.SemaphoreType.DMA((N_ARRIVALS,)),
            pltpu.SemaphoreType.REGULAR((1,)),
            *stage(16, 512),
            *stage(64, 128),
        ],
        compiler_params=pltpu.CompilerParams(
            collective_id=0, has_side_effects=True, vmem_limit_bytes=58 * 2**20
        ),
        name="hamiltonian",
    )(wave_t.reshape(2, 4, 2, 2, 16, 512), left_ops, right_ops, pattern, sector_size)
    first, second = pl.pallas_call(
        hand_over,
        out_shape=(out, out),
        in_specs=[hbm, hbm],
        out_specs=(hbm, hbm),
        scratch_shapes=[pltpu.SemaphoreType.DMA((8,))],
        name="hand_over",
    )(first, second)
    return first.reshape(16, 32, 512), second.reshape(16, 32, 512)


def solution(mesh):
    return jax.shard_map(
        on_device,
        mesh=mesh,
        in_specs=(
            P(None, "sec", None),
            P("ops", None, None),
            P("ops", None, None),
            P("ops", None),
            P(),
        ),
        out_specs=(P(None, "sec", None), P(None, "sec", None)),
        check_vma=False,
    )
```

```python
import jax
import jax.numpy as jnp
from jax import lax
from jax.experimental import pallas as pl
from jax.experimental.pallas import tpu as pltpu
from jax.sharding import PartitionSpec as P

MESH = pl.DeviceIdType.MESH
BF = jnp.bfloat16
F32 = jnp.float32
NT = (((1,), (1,)), ((), ()))
NN = (((1,), (0,)), ((), ()))
N_STAGE = 14
N_ARRIVALS = 106
N_SENDS = 56


def dot(a, b, dims):
    return lax.dot_general(a, b, dims, preferred_element_type=F32)


def kernel(wave, lops, rops, pat, sizes, out1, out2, *scratch):
    wbuf, lf, rf, rsel, lsel, va, vb, mid, f2, obuf, lsem, ssem, rsem, relay = scratch[: -2 * N_STAGE]
    stage1, stage2 = scratch[-2 * N_STAGE : -N_STAGE], scratch[-N_STAGE:]
    ops, sec = lax.axis_index("ops"), lax.axis_index("sec")
    x, zh, c = ops // 8, (ops // 2) % 4, ops % 2
    zl, y = sec // 4, sec % 4
    z = zh * 4 + zl

    def to_x(d):
        return {"ops": ((x + d) % 4 * 4 + zh) * 2 + c, "sec": sec}

    def to_y(d):
        return {"ops": ops, "sec": zl * 4 + (y + d) % 4}

    def to_z(d):
        w = (z + d + 16) % 16
        return {"ops": (x * 4 + w // 4) * 2 + c, "sec": w % 4 * 4 + y}

    other = {"ops": ops + 1 - 2 * c, "sec": sec}

    sent = []
    count = [0]

    def copies(n):
        first = count[0]
        count[0] += n
        return first

    def send_all(group, total):
        i = len(sent)
        assert i < N_SENDS, i
        for src, dst, index, device in group:
            pltpu.make_async_remote_copy(
                src_ref=src, dst_ref=dst, send_sem=ssem.at[i], recv_sem=rsem.at[index],
                device_id=device, device_id_type=MESH,
            ).start()
        sent.append(pltpu.make_async_copy(total, total, ssem.at[i]))

    def send(src, dst, index, device):
        send_all([(src, dst, index, device)], src)

    def drain():
        while sent:
            sent.pop().wait()

    def arrived(ref, index):
        pltpu.make_async_copy(ref, ref, rsem.at[index]).wait()

    load_w = pltpu.make_async_copy(wave, wbuf, lsem.at[0])
    load_r = pltpu.make_async_copy(rops, rf, lsem.at[1])
    load_l = pltpu.make_async_copy(lops, lf, lsem.at[2])
    load_w.start()
    load_r.start()
    load_l.start()
    partners = [other] + [to_y(d) for d in (1, 2, 3)] + [to_x(d) for d in (1, 2, 3)] + [to_z(d) for d in (1, 2, -2, -1)]
    barrier = pltpu.get_barrier_semaphore()
    for device in partners:
        pl.semaphore_signal(barrier, inc=1, device_id=device, device_id_type=MESH)

    load_w.wait()
    row = lax.broadcasted_iota(jnp.int32, (16, 512), 0) + (zl * 128 + y * 32)
    col = lax.broadcasted_iota(jnp.int32, (16, 512), 1)

    def mask_wave(k, carry):
        cc, xx = k // 4, k % 4
        for rh in range(2):
            edge = jnp.maximum(row + 16 * rh, col)
            for bp in range(2):
                block = wbuf[cc, xx, bp, rh].astype(F32)
                va[zl, cc, xx, rh, bp] = jnp.where(edge < sizes[2 * k + bp], block, 0.0).astype(BF)
        return carry

    lax.fori_loop(0, 8, mask_wave, 0)
    pl.semaphore_wait(barrier, len(partners))
    for d in (2, -2):
        pl.semaphore_signal(relay.at[0], inc=1, device_id=to_z(d), device_id_type=MESH)

    z_of = [zl, (zl + 3) % 4, (zl + 1) % 4, (zl + 2) % 4]
    x_of = [x, (x + 3) % 4, (x + 1) % 4, (x + 2) % 4]
    step = [0, 1, 3, 2]

    def gather(v, chunk, whole_slab):
        halves = (0, 1) if chunk is None else (chunk,)
        rows = pl.ds(halves[0], len(halves))
        a1, b1, a2, b2, cx = copies(4), copies(3), copies(4), copies(4), copies(1)

        def z_send(xx, bp, i0):
            block = v.at[zl, c, xx, rows, bp]
            group = [(block, block, i0, to_z(1)), (block, block, i0 + 1, to_z(-1))]
            for rh in halves:
                part = v.at[zl, c, xx, rh, bp]
                group.append((part, part, i0 + 2 + rh, to_z(2 - 4 * rh)))
            send_all(group, v.at[zl, c, pl.ds(0, 3), rows, bp])

        def z_arrived(xx, bp, k, i0):
            if k < 3:
                arrived(v.at[z_of[k], c, xx, rows, bp], i0 + k - 1)
            else:
                for rh in halves:
                    arrived(v.at[z_of[k], c, xx, rh, bp], i0 + 2 + rh)

        def x_send(zz, bp, indices):
            block = v.at[zz, c, x, rows, bp]
            group = [(block, block, i, to_x(d)) for d, i in zip((1, 2, 3), indices)]
            send_all(group, v.at[zz, c, pl.ds(0, 3), rows, bp])

        z_send(x, 0, a1)
        if whole_slab:
            for k in range(4):
                z_send(x_of[k], 1, b2)
        else:
            x_send(zl, 1, (b1, b1 + 1, b1 + 2))
            x_send(zl, 0, (a2, a2, a2))
            z_send(x, 1, b2)
        yield
        for k in (1, 2, 3):
            if not whole_slab:
                arrived(v.at[zl, c, x_of[k], rows, 1], b1 + step[k] - 1)
                z_send(x_of[k], 1, b2)
            z_arrived(x, 0, k, a1)
            x_send(z_of[k], 0, (a2 + k, a2 + k, a2 + k))
        yield
        for k in range(4):
            if k == 0 and whole_slab:
                continue
            arrived(v.at[z_of[k], c, pl.ds(0, 3), rows, 0], a2 + k)
            if k > 0:
                z_arrived(slice(None), 1, k, b2)
            block = v.at[z_of[k], c, :, rows]
            send(block, block, cx, other)
        yield
        arrived(v.at[pl.ds(0, 3 if whole_slab else 4), 1 - c, :, rows], cx)
        yield

    def run(flows, steps):
        for _ in range(steps):
            for flow in flows:
                next(flow)

    def reduce(pair, half, finish, s0s, s0r, s0, r1y, r1x, t1, t2, t2b, r2x, r2y, wb, z1, sb, z2):
        pair_z = 4 - 8 * (zh % 2)
        p0, py, px, qx, qy, p3 = copies(4), copies(4), copies(2), copies(2), copies(2), copies(8)
        def theirs(k):
            s0s[k] = pair(1 - c, (x + k + 1) % 4).astype(BF)
            send(s0s.at[k], s0r.at[k], p0 + k, other)

        def first_sends(k, ch):
            if k < 3:
                send(s0.at[k, ch, 1], r1x.at[ch, k], px + ch, to_x(k + 1))
            if k % 2:
                two = pl.ds(k - 1, 2)
                group = [
                    (s0.at[two, ch, 0, (y + e) % 4], r1y.at[ch, e - 1, two], py + 2 * ch + k // 2, to_y(e)) for e in (1, 2, 3)
                ]
                send_all(group, r1y.at[ch, :, two])

        def ours(k):
            total = pair(c, (x + k + 1) % 4)
            arrived(s0r.at[k], p0 + k)
            total = total + s0r[k].astype(F32)
            for ch in range(2):
                for bp in range(2):
                    s0[k, ch, bp] = total[bp, :, ch * half : (ch + 1) * half].astype(BF)
            first_sends(k, 0)

        for k in (0, 1, 2):
            theirs(k)
        ours(0)
        theirs(3)
        for k in (1, 2, 3):
            ours(k)
        for k in range(4):
            first_sends(k, 1)

        def flow(ch):
            def sum_t1(k):
                total = s0[k, ch, 0, y].astype(F32)
                for e in (1, 2, 3):
                    total = total + r1y[ch, e - 1, k].astype(F32)
                return total

            for k in range(4):
                if k % 2 == 0:
                    arrived(r1y.at[ch, :, pl.ds(k, 2)], py + 2 * ch + k // 2)
                if k < 3:
                    t1[ch, k] = sum_t1(k).astype(BF)
                    if k == 2:
                        group = [(t1.at[ch, m], r2x.at[ch, m], qx + ch, to_x(m + 1)) for m in range(3)]
                        send_all(group, r2x.at[ch])
            arrived(r1x.at[ch], px + ch)
            mine = s0[3, ch, 1].astype(F32)
            for k in range(3):
                mine = mine + r1x[ch, k].astype(F32)
            t2[ch] = mine
            for e in (1, 2, 3):
                q = (y + e) % 4
                t2b[ch, e - 1] = t2[ch, q].astype(BF)
            group = [(t2b.at[ch, e - 1], r2y.at[ch, e - 1], qy + ch, to_y(e)) for e in (1, 2, 3)]
            send_all(group, r2y.at[ch])
            yield
            w0 = sum_t1(3)
            arrived(r2x.at[ch], qx + ch)
            for k in range(3):
                w0 = w0 + r2x[ch, k].astype(F32)
            wb[ch, 0] = w0.astype(BF)
            send(wb.at[ch, 0], z1.at[ch, 0], p3 + 4 * ch, to_z(pair_z))
            w1 = t2[ch, y]
            arrived(r2y.at[ch], qy + ch)
            for k in range(3):
                w1 = w1 + r2y[ch, k].astype(F32)
            wb[ch, 1] = w1.astype(BF)
            send(wb.at[ch, 1], z1.at[ch, 1], p3 + 4 * ch + 1, to_z(-pair_z))
            yield
            for bp, d in ((0, -pair_z), (1, pair_z)):
                arrived(z1.at[ch, bp], p3 + 4 * ch + bp)
                sb[ch, bp] = (wb[ch, bp].astype(F32) + z1[ch, bp].astype(F32)).astype(BF)
                send(sb.at[ch, bp], z2.at[ch, bp], p3 + 4 * ch + 2 + bp, to_z(d))
            yield
            for bp in range(2):
                arrived(z2.at[ch, bp], p3 + 4 * ch + 2 + bp)
            yield from finish(ch, [sb[ch, bp].astype(F32) + z2[ch, bp].astype(F32) for bp in range(2)])

        return [flow(0), flow(1)]

    def pick(shape, kdim):
        k = lax.broadcasted_iota(jnp.int32, shape, kdim)
        m = lax.broadcasted_iota(jnp.int32, shape, 1 - kdim)
        return jnp.where(k == m // 32 * 128 + y * 32 + m % 32, 1.0, 0.0).astype(BF)

    start = gather(va, None, True)
    next(start)
    next(start)
    load_r.wait()
    load_l.wait()
    pick_t = pick((128, 512), 1)
    for t in range(3):
        rsel[pl.ds(128 * t, 128)] = dot(pick_t, rf[t], NT).astype(BF)
    next(start)

    def left_half(cc):
        lrows = jnp.concatenate([lf[t, pl.ds(zl * 128, 128)] for t in range(3)], axis=0)

        def body(xx, carry):
            src = [va[:, cc, xx, :, bp].reshape(128, 512) for bp in range(2)]
            res = dot(lrows, jnp.concatenate(src, axis=0), NT).astype(BF)
            for t in range(3):
                for bp in range(2):
                    mid[t, cc * 8 + xx * 2 + bp] = res[128 * t : 128 * t + 128, 128 * bp : 128 * bp + 128]
            return carry

        lax.fori_loop(0, 4, body, 0)

    left_half(c)
    next(start)
    left_half(1 - c)
    pl.semaphore_wait(relay.at[0], 2)

    def pair1(cc, xx):
        rows = []
        for bp in range(2):
            b = cc * 8 + xx * 2 + bp
            rows.append(jnp.concatenate([mid[t, pat[t, b]] for t in range(3)], axis=1))
        res = dot(jnp.concatenate(rows, axis=0), rsel[...], NN)
        return res.reshape(2, 4, 32, 512)

    def finish1(ch, totals):
        rr = lax.broadcasted_iota(jnp.int32, (16, 512), 0) + (zl * 128 + y * 32 + 16 * ch)
        edge = jnp.maximum(rr, lax.broadcasted_iota(jnp.int32, (16, 512), 1))
        for bp in range(2):
            vb[zl, c, x, ch, bp] = jnp.where(edge < sizes[c * 8 + x * 2 + bp], totals[bp], 0.0).astype(BF)
        yield from gather(vb, ch, False)

    flows = reduce(pair1, 16, finish1, *stage1)
    pick_n = pick((512, 128), 0)
    run(flows, 2)
    drain()
    for t in range(3):
        chosen = dot(lf[t], pick_n, NN).astype(BF)
        for zz in range(4):
            for q in range(4):
                for rh in range(2):
                    a = zz * 128 + q * 32 + rh * 16
                    b = q * 128 + rh * 64 + zz * 16
                    lsel[b : b + 16, 128 * t : 128 * t + 128] = chosen[a : a + 16]
    run(flows, 4)

    def right_half(cc):
        rrows = jnp.concatenate([rf[t, pl.ds(zl * 128, 128)] for t in range(3)], axis=0)

        def body(xx, carry):
            src = [vb[:, cc, xx, :, bp].reshape(128, 512) for bp in range(2)]
            res = dot(jnp.concatenate(src, axis=0), rrows, NT).astype(BF)
            for t in range(3):
                for bp in range(2):
                    mid[t, cc * 8 + xx * 2 + bp] = res[128 * bp : 128 * bp + 128, 128 * t : 128 * t + 128]
            return carry

        lax.fori_loop(0, 4, body, 0)

    right_half(c)
    run(flows, 1)
    stores = []

    def store(src, dst, index):
        for rh in range(2):
            for bp in range(2):
                cp = pltpu.make_async_copy(src.at[:, :, rh, bp], dst.at[:, :, bp, rh], lsem.at[index + 2 * rh + bp])
                cp.start()
                stores.append(cp)

    store(vb.at[zl], out1, 5)
    right_half(1 - c)

    def pair2(cc, xx):
        cols = []
        for bp in range(2):
            b = cc * 8 + xx * 2 + bp
            cols.append(jnp.concatenate([mid[t, pat[t, b]] for t in range(3)], axis=0))
        res = dot(lsel[...], jnp.concatenate(cols, axis=1), NN)
        return jnp.stack([res[:, :128].reshape(4, 128, 128), res[:, 128:].reshape(4, 128, 128)])

    def lanes(zz):
        return pl.ds(pl.multiple_of(zz * 128, 128), 128)

    def finish2(ch, totals):
        shape = (4, 16, 128)
        rr = lax.broadcasted_iota(jnp.int32, shape, 0) * 128 + lax.broadcasted_iota(jnp.int32, shape, 1)
        edge = jnp.maximum(rr + (y * 32 + 16 * ch), lax.broadcasted_iota(jnp.int32, shape, 2) + zl * 128)
        for bp in range(2):
            f2[ch, bp] = jnp.where(edge < sizes[c * 8 + x * 2 + bp], totals[bp].reshape(shape), 0.0).astype(BF)
        here = obuf.at[c, x, ch, :, :, lanes(zl)]
        own = pltpu.make_async_copy(f2.at[ch, :, zl], here, lsem.at[3 + ch])
        own.start()
        g2 = copies(3)
        away = (1, -1, 2 - 4 * ch)
        for k, d in enumerate(away):
            send(f2.at[ch, :, (zl + d + 4) % 4], here, g2 + k, to_z(d))
        yield
        own.wait()
        for k, d in enumerate(away):
            arrived(obuf.at[c, x, ch, :, :, lanes((zl - d + 4) % 4)], g2 + k)
        gx, gc = copies(3), copies(1)
        block = obuf.at[c, x, ch]
        send_all([(block, block, gx + d - 1, to_x(d)) for d in (1, 2, 3)], obuf.at[c, pl.ds(0, 3), ch])
        send(block, block, gc, other)
        yield
        for d in (1, 3, 2):
            block = obuf.at[c, (x + 4 - d) % 4, ch]
            arrived(block, gx + d - 1)
            send(block, block, gc, other)
        yield
        arrived(obuf.at[1 - c, :, ch], gc)
        yield

    flows = reduce(pair2, 64, finish2, *stage2)
    run(flows, 2)
    drain()
    run(flows, 5)
    store(obuf, out2, 11)
    drain()
    for cp in stores:
        cp.wait()
    assert count[0] == N_ARRIVALS, count


def hand_over(first, second, out1, out2, held, sem):
    steps = []
    for i, (src, dst) in enumerate(((first, out1), (second, out2))):
        for k in range(4):
            part = pl.ds(4 * k, 4)
            load = pltpu.make_async_copy(src.at[part], held.at[i, part], sem.at[i, k, 0])
            load.start()
            steps.append((load, pltpu.make_async_copy(held.at[i, part], dst.at[part], sem.at[i, k, 1])))
    for load, store in steps:
        load.wait()
        store.start()
    for _, store in steps:
        store.wait()


def on_device(wave_t, left_ops, right_ops, pattern, sector_size):
    def stage(r, w):
        return [
            pltpu.VMEM((4, 2, 4, 2 * r, w), BF),
            pltpu.VMEM((4, 2, 4, 2 * r, w), BF),
            pltpu.VMEM((4, 2, 2, 4, r, w), BF),
            pltpu.VMEM((2, 3, 4, r, w), BF),
            pltpu.VMEM((2, 3, 4, r, w), BF),
            pltpu.VMEM((2, 3, r, w), BF),
            pltpu.VMEM((2, 4, r, w), F32),
            pltpu.VMEM((2, 3, r, w), BF),
            pltpu.VMEM((2, 3, r, w), BF),
            pltpu.VMEM((2, 3, r, w), BF),
            pltpu.VMEM((2, 2, r, w), BF),
            pltpu.VMEM((2, 2, r, w), BF),
            pltpu.VMEM((2, 2, r, w), BF),
            pltpu.VMEM((2, 2, r, w), BF),
        ]

    hbm = pl.BlockSpec(memory_space=pl.ANY)
    smem = pl.BlockSpec(memory_space=pltpu.SMEM)
    out = jax.ShapeDtypeStruct((2, 4, 2, 2, 16, 512), BF)
    first, second = pl.pallas_call(
        kernel,
        out_shape=(out, out),
        in_specs=[hbm, hbm, hbm, smem, smem],
        out_specs=(hbm, hbm),
        scratch_shapes=[
            pltpu.VMEM((2, 4, 2, 2, 16, 512), BF),
            pltpu.VMEM((3, 512, 512), BF),
            pltpu.VMEM((3, 512, 512), BF),
            pltpu.VMEM((384, 512), BF),
            pltpu.VMEM((512, 384), BF),
            pltpu.VMEM((4, 2, 4, 2, 2, 16, 512), BF),
            pltpu.VMEM((4, 2, 4, 2, 2, 16, 512), BF),
            pltpu.VMEM((3, 16, 128, 128), BF),
            pltpu.VMEM((2, 2, 4, 16, 128), BF),
            pltpu.VMEM((2, 4, 2, 2, 16, 512), BF),
            pltpu.SemaphoreType.DMA((16,)),
            pltpu.SemaphoreType.DMA((N_SENDS,)),
            pltpu.SemaphoreType.DMA((N_ARRIVALS,)),
            pltpu.SemaphoreType.REGULAR((1,)),
            *stage(16, 512),
            *stage(64, 128),
        ],
        compiler_params=pltpu.CompilerParams(
            collective_id=0, has_side_effects=True, vmem_limit_bytes=58 * 2**20
        ),
        name="hamiltonian",
    )(wave_t.reshape(2, 4, 2, 2, 16, 512), left_ops, right_ops, pattern, sector_size)
    result = jax.ShapeDtypeStruct((16, 32, 512), BF)
    return pl.pallas_call(
        hand_over,
        out_shape=(result, result),
        in_specs=[hbm, hbm],
        out_specs=(hbm, hbm),
        scratch_shapes=[pltpu.VMEM((2, 16, 32, 512), BF), pltpu.SemaphoreType.DMA((2, 4, 2))],
        compiler_params=pltpu.CompilerParams(vmem_limit_bytes=58 * 2**20),
        name="hand_over",
    )(first.reshape(16, 32, 512), second.reshape(16, 32, 512))


def solution(mesh):
    return jax.shard_map(
        on_device,
        mesh=mesh,
        in_specs=(
            P(None, "sec", None),
            P("ops", None, None),
            P("ops", None, None),
            P("ops", None),
            P(),
        ),
        out_specs=(P(None, "sec", None), P(None, "sec", None)),
        check_vma=False,
    )
```

```python
import jax
import jax.numpy as jnp
from jax import lax
from jax.experimental import pallas as pl
from jax.experimental.pallas import tpu as pltpu
from jax.sharding import PartitionSpec as P

MESH = pl.DeviceIdType.MESH
BF = jnp.bfloat16
F32 = jnp.float32
NT = (((1,), (1,)), ((), ()))
NN = (((1,), (0,)), ((), ()))
N_STAGE = 14
N_ARRIVALS = 99
N_SENDS = 60


def dot(a, b, dims):
    return lax.dot_general(a, b, dims, preferred_element_type=F32)


def kernel(wave, lops, rops, pat, sizes, out1, out2, *scratch):
    wbuf, lf, rf, rsel, lsel, va, vb, mid, f2, obuf, lsem, ssem, rsem, relay = scratch[: -2 * N_STAGE]
    stage1, stage2 = scratch[-2 * N_STAGE : -N_STAGE], scratch[-N_STAGE:]
    ops, sec = lax.axis_index("ops"), lax.axis_index("sec")
    x, zh, c = ops // 8, (ops // 2) % 4, ops % 2
    zl, y = sec // 4, sec % 4
    z = zh * 4 + zl

    def to_x(d):
        return {"ops": ((x + d) % 4 * 4 + zh) * 2 + c, "sec": sec}

    def to_y(d):
        return {"ops": ops, "sec": zl * 4 + (y + d) % 4}

    def to_z(d):
        w = (z + d + 16) % 16
        return {"ops": (x * 4 + w // 4) * 2 + c, "sec": w % 4 * 4 + y}

    def to_xz(dx, d):
        w = (z + d + 16) % 16
        return {"ops": ((x + dx) % 4 * 4 + w // 4) * 2 + c, "sec": w % 4 * 4 + y}

    other = {"ops": ops + 1 - 2 * c, "sec": sec}

    sent = []
    count = [0]

    def copies(n):
        first = count[0]
        count[0] += n
        return first

    def send_all(group, total):
        i = len(sent)
        assert i < N_SENDS, i
        for src, dst, index, device in group:
            pltpu.make_async_remote_copy(
                src_ref=src, dst_ref=dst, send_sem=ssem.at[i], recv_sem=rsem.at[index],
                device_id=device, device_id_type=MESH,
            ).start()
        sent.append(pltpu.make_async_copy(total, total, ssem.at[i]))

    def send(src, dst, index, device):
        send_all([(src, dst, index, device)], src)

    def drain():
        while sent:
            sent.pop().wait()

    def arrived(ref, index):
        pltpu.make_async_copy(ref, ref, rsem.at[index]).wait()

    load_w = pltpu.make_async_copy(wave, wbuf, lsem.at[0])
    load_r = pltpu.make_async_copy(rops, rf, lsem.at[1])
    load_l = pltpu.make_async_copy(lops, lf, lsem.at[2])
    load_w.start()
    load_r.start()
    load_l.start()
    partners = [other] + [to_y(d) for d in (1, 2, 3)] + [to_x(d) for d in (1, 2, 3)] + [to_z(d) for d in (1, 2, -2, -1)]
    barrier = pltpu.get_barrier_semaphore()
    for device in partners:
        pl.semaphore_signal(barrier, inc=1, device_id=device, device_id_type=MESH)

    load_w.wait()
    row = lax.broadcasted_iota(jnp.int32, (16, 512), 0) + (zl * 128 + y * 32)
    col = lax.broadcasted_iota(jnp.int32, (16, 512), 1)

    def mask_wave(k, carry):
        cc, xx = k // 4, k % 4
        for rh in range(2):
            edge = jnp.maximum(row + 16 * rh, col)
            for bp in range(2):
                block = wbuf[cc, xx, bp, rh].astype(F32)
                va[zl, cc, xx, rh, bp] = jnp.where(edge < sizes[2 * k + bp], block, 0.0).astype(BF)
        return carry

    lax.fori_loop(0, 8, mask_wave, 0)
    pl.semaphore_wait(barrier, len(partners))
    for d in (2, -2):
        pl.semaphore_signal(relay.at[0], inc=1, device_id=to_z(d), device_id_type=MESH)

    z_of = [zl, (zl + 3) % 4, (zl + 1) % 4, (zl + 2) % 4]
    x_of = [x, (x + 3) % 4, (x + 1) % 4, (x + 2) % 4]
    step = [0, 1, 3, 2]

    def gather(v, chunk, whole_slab):
        halves = (0, 1) if chunk is None else (chunk,)
        rows = pl.ds(halves[0], len(halves))
        a1, b1, a2, b2, cx = copies(4), copies(3), copies(4), copies(4), copies(2)

        def z_send(xx, bp, i0):
            block = v.at[zl, c, xx, rows, bp]
            group = [(block, block, i0, to_z(1)), (block, block, i0 + 1, to_z(-1))]
            for rh in halves:
                part = v.at[zl, c, xx, rh, bp]
                group.append((part, part, i0 + 2 + rh, to_z(2 - 4 * rh)))
            send_all(group, v.at[zl, c, pl.ds(0, 3), rows, bp])

        def z_arrived(xx, bp, k, i0):
            if k < 3:
                arrived(v.at[z_of[k], c, xx, rows, bp], i0 + k - 1)
            else:
                for rh in halves:
                    arrived(v.at[z_of[k], c, xx, rh, bp], i0 + 2 + rh)

        def x_send(zz, bp, indices):
            block = v.at[zz, c, x, rows, bp]
            group = [(block, block, i, to_x(d)) for d, i in zip((1, 2, 3), indices)]
            send_all(group, v.at[zz, c, pl.ds(0, 3), rows, bp])

        z_send(x, 0, a1)
        if whole_slab:
            for k in range(4):
                z_send(x_of[k], 1, b2)
        else:
            x_send(zl, 1, (b1, b1 + 1, b1 + 2))
            x_send(zl, 0, (a2, a2, a2))
            z_send(x, 1, b2)
        yield
        for k in (1, 2, 3):
            if not whole_slab:
                arrived(v.at[zl, c, x_of[k], rows, 1], b1 + step[k] - 1)
                z_send(x_of[k], 1, b2)
            z_arrived(x, 0, k, a1)
            x_send(z_of[k], 0, (a2 + k, a2 + k, a2 + k))
        yield
        if whole_slab:
            for k in (1, 2, 3):
                z_arrived(slice(None), 1, k, b2)
                block = v.at[z_of[k], c, :, :, 1]
                send(block, block, cx, other)
            yield
            for k in (1, 2, 3):
                arrived(v.at[z_of[k], c, pl.ds(0, 3), rows, 0], a2 + k)
                block = v.at[z_of[k], c, :, :, 0]
                send(block, block, cx + 1, other)
            yield
            for i in range(2):
                arrived(v.at[pl.ds(0, 3), 1 - c, :, :, 0], cx + i)
                yield
            return
        for k in range(4):
            arrived(v.at[z_of[k], c, pl.ds(0, 3), rows, 0], a2 + k)
            if k > 0:
                z_arrived(slice(None), 1, k, b2)
            block = v.at[z_of[k], c, :, rows]
            send(block, block, cx, other)
        yield
        arrived(v.at[:, 1 - c, :, rows], cx)
        yield

    def run(flows, steps):
        for _ in range(steps):
            for flow in flows:
                next(flow)

    def reduce(pair, half, finish, s0s, s0r, s0, r1y, r1x, t1, t2, t2b, r2x, r2y, wb, z1, sb, z2):
        pair_z = 4 - 8 * (zh % 2)
        p0, py, px, qx, qy, p3 = copies(4), copies(4), copies(2), copies(2), copies(2), copies(8)
        def theirs(k):
            s0s[k] = pair(1 - c, (x + k + 1) % 4).astype(BF)
            send(s0s.at[k], s0r.at[k], p0 + k, other)

        def first_sends(k, ch):
            if k < 3:
                send(s0.at[k, ch, 1], r1x.at[ch, k], px + ch, to_x(k + 1))
            if k % 2:
                two = pl.ds(k - 1, 2)
                group = [
                    (s0.at[two, ch, 0, (y + e) % 4], r1y.at[ch, e - 1, two], py + 2 * ch + k // 2, to_y(e)) for e in (1, 2, 3)
                ]
                send_all(group, r1y.at[ch, :, two])

        def ours(k):
            total = pair(c, (x + k + 1) % 4)
            arrived(s0r.at[k], p0 + k)
            total = total + s0r[k].astype(F32)
            for ch in range(2):
                for bp in range(2):
                    s0[k, ch, bp] = total[bp, :, ch * half : (ch + 1) * half].astype(BF)
            first_sends(k, 0)

        for k in (0, 1, 2):
            theirs(k)
        ours(0)
        theirs(3)
        for k in (1, 2, 3):
            ours(k)
        for k in range(4):
            first_sends(k, 1)

        def flow(ch):
            def sum_t1(k):
                total = s0[k, ch, 0, y].astype(F32)
                for e in (1, 2, 3):
                    total = total + r1y[ch, e - 1, k].astype(F32)
                return total

            for k in range(4):
                if k % 2 == 0:
                    arrived(r1y.at[ch, :, pl.ds(k, 2)], py + 2 * ch + k // 2)
                if k < 3:
                    t1[ch, k] = sum_t1(k).astype(BF)
                    if k == 2:
                        group = [(t1.at[ch, m], r2x.at[ch, m], qx + ch, to_x(m + 1)) for m in range(3)]
                        send_all(group, r2x.at[ch])
            arrived(r1x.at[ch], px + ch)
            mine = s0[3, ch, 1].astype(F32)
            for k in range(3):
                mine = mine + r1x[ch, k].astype(F32)
            t2[ch] = mine
            for e in (1, 2, 3):
                q = (y + e) % 4
                t2b[ch, e - 1] = t2[ch, q].astype(BF)
            group = [(t2b.at[ch, e - 1], r2y.at[ch, e - 1], qy + ch, to_y(e)) for e in (1, 2, 3)]
            send_all(group, r2y.at[ch])
            yield
            w0 = sum_t1(3)
            arrived(r2x.at[ch], qx + ch)
            for k in range(3):
                w0 = w0 + r2x[ch, k].astype(F32)
            wb[ch, 0] = w0.astype(BF)
            send(wb.at[ch, 0], z1.at[ch, 0], p3 + 4 * ch, to_z(pair_z))
            w1 = t2[ch, y]
            arrived(r2y.at[ch], qy + ch)
            for k in range(3):
                w1 = w1 + r2y[ch, k].astype(F32)
            wb[ch, 1] = w1.astype(BF)
            send(wb.at[ch, 1], z1.at[ch, 1], p3 + 4 * ch + 1, to_z(-pair_z))
            yield
            for bp, d in ((0, -pair_z), (1, pair_z)):
                arrived(z1.at[ch, bp], p3 + 4 * ch + bp)
                sb[ch, bp] = (wb[ch, bp].astype(F32) + z1[ch, bp].astype(F32)).astype(BF)
                send(sb.at[ch, bp], z2.at[ch, bp], p3 + 4 * ch + 2 + bp, to_z(d))
            yield
            for bp in range(2):
                arrived(z2.at[ch, bp], p3 + 4 * ch + 2 + bp)
            yield from finish(ch, [sb[ch, bp].astype(F32) + z2[ch, bp].astype(F32) for bp in range(2)])

        return [flow(0), flow(1)]

    def pick(shape, kdim):
        k = lax.broadcasted_iota(jnp.int32, shape, kdim)
        m = lax.broadcasted_iota(jnp.int32, shape, 1 - kdim)
        return jnp.where(k == m // 32 * 128 + y * 32 + m % 32, 1.0, 0.0).astype(BF)

    start = gather(va, None, True)
    next(start)
    next(start)
    load_r.wait()
    load_l.wait()
    pick_t = pick((128, 512), 1)
    for t in range(3):
        rsel[pl.ds(128 * t, 128)] = dot(pick_t, rf[t], NT).astype(BF)
    next(start)

    def left_part(cc, bp):
        lrows = jnp.concatenate([lf[t, pl.ds(zl * 128, 128)] for t in range(3)], axis=0)

        def body(k, carry):
            src = [va[:, cc, 2 * k + i, :, bp].reshape(128, 512) for i in range(2)]
            res = dot(lrows, jnp.concatenate(src, axis=0), NT).astype(BF)
            for t in range(3):
                for i in range(2):
                    block = res[128 * t : 128 * t + 128, 128 * i : 128 * i + 128]
                    mid[t, cc * 8 + (2 * k + i) * 2 + bp] = block.reshape(4, 2, 16, 128)
            return carry

        lax.fori_loop(0, 2, body, 0)

    left_part(c, 1)
    next(start)
    left_part(c, 0)
    next(start)
    left_part(1 - c, 1)
    next(start)
    left_part(1 - c, 0)
    pl.semaphore_wait(relay.at[0], 2)

    def pair1(cc, xx):
        rows = []
        for bp in range(2):
            b = cc * 8 + xx * 2 + bp
            rows.append(jnp.concatenate([mid[t, pat[t, b]].reshape(128, 128) for t in range(3)], axis=1))
        res = dot(jnp.concatenate(rows, axis=0), rsel[...], NN)
        return res.reshape(2, 4, 32, 512)

    def finish1(ch, totals):
        rr = lax.broadcasted_iota(jnp.int32, (16, 512), 0) + (zl * 128 + y * 32 + 16 * ch)
        edge = jnp.maximum(rr, lax.broadcasted_iota(jnp.int32, (16, 512), 1))
        for bp in range(2):
            vb[zl, c, x, ch, bp] = jnp.where(edge < sizes[c * 8 + x * 2 + bp], totals[bp], 0.0).astype(BF)
        yield from gather(vb, ch, False)

    flows = reduce(pair1, 16, finish1, *stage1)
    pick_n = pick((512, 128), 0)
    run(flows, 2)
    drain()
    for t in range(3):
        chosen = dot(lf[t], pick_n, NN).astype(BF)
        for zz in range(4):
            for q in range(4):
                for rh in range(2):
                    a = zz * 128 + q * 32 + rh * 16
                    b = q * 128 + rh * 64 + zz * 16
                    lsel[b : b + 16, 128 * t : 128 * t + 128] = chosen[a : a + 16]
    run(flows, 3)

    def right_part(cc, ch):
        rrows = jnp.concatenate([rf[t, pl.ds(zl * 128, 128)] for t in range(3)], axis=0)
        res = dot(vb[:, cc, :, ch].reshape(512, 512), rrows, NT).astype(BF).reshape(4, 8, 16, 384)
        for t in range(3):
            for zz in range(4):
                mid[t, pl.ds(cc * 8, 8), zz, ch] = res[zz, :, :, 128 * t : 128 * t + 128]

    for ch in range(2):
        next(flows[ch])
        right_part(c, ch)
        next(flows[ch])
        right_part(1 - c, ch)
    stores = []

    def store(src, dst, index):
        for rh in range(2):
            for bp in range(2):
                cp = pltpu.make_async_copy(src.at[:, :, rh, bp], dst.at[:, :, bp, rh], lsem.at[index + 2 * rh + bp])
                cp.start()
                stores.append(cp)

    store(vb.at[zl], out1, 5)

    def pair2(cc, xx):
        cols = []
        for bp in range(2):
            b = cc * 8 + xx * 2 + bp
            cols.append(jnp.concatenate([mid[t, pat[t, b]].reshape(128, 128) for t in range(3)], axis=0))
        res = dot(lsel[...], jnp.concatenate(cols, axis=1), NN)
        return jnp.stack([res[:, :128].reshape(4, 128, 128), res[:, 128:].reshape(4, 128, 128)])

    def lanes(zz):
        return pl.ds(pl.multiple_of(zz * 128, 128), 128)

    def finish2(ch, totals):
        shape = (4, 16, 128)
        rr = lax.broadcasted_iota(jnp.int32, shape, 0) * 128 + lax.broadcasted_iota(jnp.int32, shape, 1)
        edge = jnp.maximum(rr + (y * 32 + 16 * ch), lax.broadcasted_iota(jnp.int32, shape, 2) + zl * 128)
        for bp in range(2):
            f2[ch, bp] = jnp.where(edge < sizes[c * 8 + x * 2 + bp], totals[bp].reshape(shape), 0.0).astype(BF)
        here = obuf.at[c, x, ch, :, :, lanes(zl)]
        g2, gc = copies(1), copies(1)
        pltpu.make_async_copy(f2.at[ch, :, zl], here, rsem.at[g2]).start()
        for d in (0, 1, -1, 2 - 4 * ch):
            group = [(f2.at[ch, :, (zl + d + 4) % 4], here, g2, to_xz(dx, d)) for dx in (0, 1, 3, 2) if d or dx]
            send_all(group, f2.at[ch, :, pl.ds(0, len(group))])
        yield
        block = obuf.at[c, :, ch]
        arrived(block, g2)
        send(block, block, gc, other)
        yield
        arrived(obuf.at[1 - c, :, ch], gc)
        yield

    flows = reduce(pair2, 64, finish2, *stage2)
    run(flows, 2)
    drain()
    run(flows, 4)
    store(obuf, out2, 11)
    drain()
    for cp in stores:
        cp.wait()
    assert count[0] == N_ARRIVALS, count


def hand_over(first, second, out1, out2, held, sem):
    steps = []
    for i, (src, dst) in enumerate(((first, out1), (second, out2))):
        for k in range(4):
            part = pl.ds(4 * k, 4)
            load = pltpu.make_async_copy(src.at[part], held.at[i, part], sem.at[i, k, 0])
            load.start()
            steps.append((load, pltpu.make_async_copy(held.at[i, part], dst.at[part], sem.at[i, k, 1])))
    for load, store in steps:
        load.wait()
        store.start()
    for _, store in steps:
        store.wait()


def on_device(wave_t, left_ops, right_ops, pattern, sector_size):
    def stage(r, w):
        return [
            pltpu.VMEM((4, 2, 4, 2 * r, w), BF),
            pltpu.VMEM((4, 2, 4, 2 * r, w), BF),
            pltpu.VMEM((4, 2, 2, 4, r, w), BF),
            pltpu.VMEM((2, 3, 4, r, w), BF),
            pltpu.VMEM((2, 3, 4, r, w), BF),
            pltpu.VMEM((2, 3, r, w), BF),
            pltpu.VMEM((2, 4, r, w), F32),
            pltpu.VMEM((2, 3, r, w), BF),
            pltpu.VMEM((2, 3, r, w), BF),
            pltpu.VMEM((2, 3, r, w), BF),
            pltpu.VMEM((2, 2, r, w), BF),
            pltpu.VMEM((2, 2, r, w), BF),
            pltpu.VMEM((2, 2, r, w), BF),
            pltpu.VMEM((2, 2, r, w), BF),
        ]

    hbm = pl.BlockSpec(memory_space=pl.ANY)
    smem = pl.BlockSpec(memory_space=pltpu.SMEM)
    out = jax.ShapeDtypeStruct((2, 4, 2, 2, 16, 512), BF)
    first, second = pl.pallas_call(
        kernel,
        out_shape=(out, out),
        in_specs=[hbm, hbm, hbm, smem, smem],
        out_specs=(hbm, hbm),
        scratch_shapes=[
            pltpu.VMEM((2, 4, 2, 2, 16, 512), BF),
            pltpu.VMEM((3, 512, 512), BF),
            pltpu.VMEM((3, 512, 512), BF),
            pltpu.VMEM((384, 512), BF),
            pltpu.VMEM((512, 384), BF),
            pltpu.VMEM((4, 2, 4, 2, 2, 16, 512), BF),
            pltpu.VMEM((4, 2, 4, 2, 2, 16, 512), BF),
            pltpu.VMEM((3, 16, 4, 2, 16, 128), BF),
            pltpu.VMEM((2, 2, 4, 16, 128), BF),
            pltpu.VMEM((2, 4, 2, 2, 16, 512), BF),
            pltpu.SemaphoreType.DMA((16,)),
            pltpu.SemaphoreType.DMA((N_SENDS,)),
            pltpu.SemaphoreType.DMA((N_ARRIVALS,)),
            pltpu.SemaphoreType.REGULAR((1,)),
            *stage(16, 512),
            *stage(64, 128),
        ],
        compiler_params=pltpu.CompilerParams(
            collective_id=0, has_side_effects=True, vmem_limit_bytes=58 * 2**20
        ),
        name="hamiltonian",
    )(wave_t.reshape(2, 4, 2, 2, 16, 512), left_ops, right_ops, pattern, sector_size)
    result = jax.ShapeDtypeStruct((16, 32, 512), BF)
    return pl.pallas_call(
        hand_over,
        out_shape=(result, result),
        in_specs=[hbm, hbm],
        out_specs=(hbm, hbm),
        scratch_shapes=[pltpu.VMEM((2, 16, 32, 512), BF), pltpu.SemaphoreType.DMA((2, 4, 2))],
        compiler_params=pltpu.CompilerParams(vmem_limit_bytes=58 * 2**20),
        name="hand_over",
    )(first.reshape(16, 32, 512), second.reshape(16, 32, 512))


def solution(mesh):
    return jax.shard_map(
        on_device,
        mesh=mesh,
        in_specs=(
            P(None, "sec", None),
            P("ops", None, None),
            P("ops", None, None),
            P("ops", None),
            P(),
        ),
        out_specs=(P(None, "sec", None), P(None, "sec", None)),
        check_vma=False,
    )
```

```python
import jax
import jax.numpy as jnp
from jax import lax
from jax.experimental import pallas as pl
from jax.experimental.pallas import tpu as pltpu
from jax.sharding import PartitionSpec as P

MESH = pl.DeviceIdType.MESH
BF = jnp.bfloat16
F32 = jnp.float32
NT = (((1,), (1,)), ((), ()))
NN = (((1,), (0,)), ((), ()))
N_STAGE = 14
N_ARRIVALS = 99
N_SENDS = 60


def dot(a, b, dims):
    return lax.dot_general(a, b, dims, preferred_element_type=F32)


def kernel(wave, lops, rops, pattern, sector, out1, obuf, *scratch):
    wbuf, lf, rf, rsel, lsel, va, vb, mid, f2, pat, sizes, lsem, ssem, rsem, relay = scratch[: -2 * N_STAGE]
    stage1, stage2 = scratch[-2 * N_STAGE : -N_STAGE], scratch[-N_STAGE:]
    ops, sec = lax.axis_index("ops"), lax.axis_index("sec")
    x, zh, c = ops // 8, (ops // 2) % 4, ops % 2
    zl, y = sec // 4, sec % 4
    z = zh * 4 + zl

    def to_x(d):
        return {"ops": ((x + d) % 4 * 4 + zh) * 2 + c, "sec": sec}

    def to_y(d):
        return {"ops": ops, "sec": zl * 4 + (y + d) % 4}

    def to_z(d):
        w = (z + d + 16) % 16
        return {"ops": (x * 4 + w // 4) * 2 + c, "sec": w % 4 * 4 + y}

    def to_xz(dx, d):
        w = (z + d + 16) % 16
        return {"ops": ((x + dx) % 4 * 4 + w // 4) * 2 + c, "sec": w % 4 * 4 + y}

    other = {"ops": ops + 1 - 2 * c, "sec": sec}

    sent = []
    count = [0]

    def copies(n):
        first = count[0]
        count[0] += n
        return first

    def send_all(group, total):
        i = len(sent)
        assert i < N_SENDS, i
        for src, dst, index, device in group:
            pltpu.make_async_remote_copy(
                src_ref=src, dst_ref=dst, send_sem=ssem.at[i], recv_sem=rsem.at[index],
                device_id=device, device_id_type=MESH,
            ).start()
        sent.append(pltpu.make_async_copy(total, total, ssem.at[i]))

    def send(src, dst, index, device):
        send_all([(src, dst, index, device)], src)

    def drain():
        while sent:
            sent.pop().wait()

    def arrived(ref, index):
        pltpu.make_async_copy(ref, ref, rsem.at[index]).wait()

    load_w = pltpu.make_async_copy(wave, wbuf, lsem.at[0])
    load_r = pltpu.make_async_copy(rops, rf, lsem.at[1])
    load_l = pltpu.make_async_copy(lops, lf, lsem.at[2])
    load_s = pltpu.make_async_copy(sector, sizes, lsem.at[3])
    load_p = pltpu.make_async_copy(pattern, pat, lsem.at[4])
    load_w.start()
    load_s.start()
    load_p.start()
    load_r.start()
    load_l.start()
    partners = [other] + [to_y(d) for d in (1, 2, 3)] + [to_x(d) for d in (1, 2, 3)] + [to_z(d) for d in (1, 2, -2, -1)]
    barrier = pltpu.get_barrier_semaphore()
    for device in partners:
        pl.semaphore_signal(barrier, inc=1, device_id=device, device_id_type=MESH)

    load_w.wait()
    load_s.wait()
    row = lax.broadcasted_iota(jnp.int32, (16, 512), 0) + (zl * 128 + y * 32)
    col = lax.broadcasted_iota(jnp.int32, (16, 512), 1)

    def mask_wave(k, carry):
        cc, xx = k // 4, k % 4
        for rh in range(2):
            edge = jnp.maximum(row + 16 * rh, col)
            for bp in range(2):
                block = wbuf[cc, xx, bp, rh].astype(F32)
                va[zl, cc, xx, rh, bp] = jnp.where(edge < sizes[2 * k + bp], block, 0.0).astype(BF)
        return carry

    lax.fori_loop(0, 8, mask_wave, 0)
    pl.semaphore_wait(barrier, len(partners))
    for d in (2, -2):
        pl.semaphore_signal(relay.at[0], inc=1, device_id=to_z(d), device_id_type=MESH)

    z_of = [zl, (zl + 3) % 4, (zl + 1) % 4, (zl + 2) % 4]
    x_of = [x, (x + 3) % 4, (x + 1) % 4, (x + 2) % 4]
    step = [0, 1, 3, 2]

    def gather(v, chunk, whole_slab):
        halves = (0, 1) if chunk is None else (chunk,)
        rows = pl.ds(halves[0], len(halves))
        a1, b1, a2, b2, cx = copies(4), copies(3), copies(4), copies(4), copies(2)

        def z_send(xx, bp, i0):
            block = v.at[zl, c, xx, rows, bp]
            group = [(block, block, i0, to_z(1)), (block, block, i0 + 1, to_z(-1))]
            for rh in halves:
                part = v.at[zl, c, xx, rh, bp]
                group.append((part, part, i0 + 2 + rh, to_z(2 - 4 * rh)))
            send_all(group, v.at[zl, c, pl.ds(0, 3), rows, bp])

        def z_arrived(xx, bp, k, i0):
            if k < 3:
                arrived(v.at[z_of[k], c, xx, rows, bp], i0 + k - 1)
            else:
                for rh in halves:
                    arrived(v.at[z_of[k], c, xx, rh, bp], i0 + 2 + rh)

        def x_send(zz, bp, indices):
            block = v.at[zz, c, x, rows, bp]
            group = [(block, block, i, to_x(d)) for d, i in zip((1, 2, 3), indices)]
            send_all(group, v.at[zz, c, pl.ds(0, 3), rows, bp])

        z_send(x, 0, a1)
        if whole_slab:
            for k in range(4):
                z_send(x_of[k], 1, b2)
        else:
            x_send(zl, 1, (b1, b1 + 1, b1 + 2))
            x_send(zl, 0, (a2, a2, a2))
            z_send(x, 1, b2)
        yield
        for k in (1, 2, 3):
            if not whole_slab:
                arrived(v.at[zl, c, x_of[k], rows, 1], b1 + step[k] - 1)
                z_send(x_of[k], 1, b2)
            z_arrived(x, 0, k, a1)
            x_send(z_of[k], 0, (a2 + k, a2 + k, a2 + k))
        yield
        if whole_slab:
            for k in (1, 2, 3):
                z_arrived(slice(None), 1, k, b2)
                block = v.at[z_of[k], c, :, :, 1]
                send(block, block, cx, other)
            yield
            for k in (1, 2, 3):
                arrived(v.at[z_of[k], c, pl.ds(0, 3), rows, 0], a2 + k)
                block = v.at[z_of[k], c, :, :, 0]
                send(block, block, cx + 1, other)
            yield
            for i in range(2):
                arrived(v.at[pl.ds(0, 3), 1 - c, :, :, 0], cx + i)
                yield
            return
        for k in range(4):
            arrived(v.at[z_of[k], c, pl.ds(0, 3), rows, 0], a2 + k)
            if k > 0:
                z_arrived(slice(None), 1, k, b2)
            block = v.at[z_of[k], c, :, rows]
            send(block, block, cx, other)
        yield
        arrived(v.at[:, 1 - c, :, rows], cx)
        yield

    def run(flows, steps):
        for _ in range(steps):
            for flow in flows:
                next(flow)

    def reduce(pair, half, finish, s0s, s0r, s0, r1y, r1x, t1, t2, t2b, r2x, r2y, wb, z1, sb, z2):
        pair_z = 4 - 8 * (zh % 2)
        p0, py, px, qx, qy, p3 = copies(4), copies(4), copies(2), copies(2), copies(2), copies(8)
        def theirs(k):
            s0s[k] = pair(1 - c, (x + k + 1) % 4).astype(BF)
            send(s0s.at[k], s0r.at[k], p0 + k, other)

        def first_sends(k, ch):
            if k < 3:
                send(s0.at[k, ch, 1], r1x.at[ch, k], px + ch, to_x(k + 1))
            if k % 2:
                two = pl.ds(k - 1, 2)
                group = [
                    (s0.at[two, ch, 0, (y + e) % 4], r1y.at[ch, e - 1, two], py + 2 * ch + k // 2, to_y(e)) for e in (1, 2, 3)
                ]
                send_all(group, r1y.at[ch, :, two])

        def ours(k):
            total = pair(c, (x + k + 1) % 4)
            arrived(s0r.at[k], p0 + k)
            total = total + s0r[k].astype(F32)
            for ch in range(2):
                for bp in range(2):
                    s0[k, ch, bp] = total[bp, :, ch * half : (ch + 1) * half].astype(BF)
            first_sends(k, 0)

        for k in (0, 1, 2):
            theirs(k)
        ours(0)
        theirs(3)
        for k in (1, 2, 3):
            ours(k)
        for k in range(4):
            first_sends(k, 1)

        def flow(ch):
            def sum_t1(k):
                total = s0[k, ch, 0, y].astype(F32)
                for e in (1, 2, 3):
                    total = total + r1y[ch, e - 1, k].astype(F32)
                return total

            for k in range(4):
                if k % 2 == 0:
                    arrived(r1y.at[ch, :, pl.ds(k, 2)], py + 2 * ch + k // 2)
                if k < 3:
                    t1[ch, k] = sum_t1(k).astype(BF)
                    if k == 2:
                        group = [(t1.at[ch, m], r2x.at[ch, m], qx + ch, to_x(m + 1)) for m in range(3)]
                        send_all(group, r2x.at[ch])
            arrived(r1x.at[ch], px + ch)
            mine = s0[3, ch, 1].astype(F32)
            for k in range(3):
                mine = mine + r1x[ch, k].astype(F32)
            t2[ch] = mine
            for e in (1, 2, 3):
                q = (y + e) % 4
                t2b[ch, e - 1] = t2[ch, q].astype(BF)
            group = [(t2b.at[ch, e - 1], r2y.at[ch, e - 1], qy + ch, to_y(e)) for e in (1, 2, 3)]
            send_all(group, r2y.at[ch])
            yield
            w0 = sum_t1(3)
            arrived(r2x.at[ch], qx + ch)
            for k in range(3):
                w0 = w0 + r2x[ch, k].astype(F32)
            wb[ch, 0] = w0.astype(BF)
            send(wb.at[ch, 0], z1.at[ch, 0], p3 + 4 * ch, to_z(pair_z))
            w1 = t2[ch, y]
            arrived(r2y.at[ch], qy + ch)
            for k in range(3):
                w1 = w1 + r2y[ch, k].astype(F32)
            wb[ch, 1] = w1.astype(BF)
            send(wb.at[ch, 1], z1.at[ch, 1], p3 + 4 * ch + 1, to_z(-pair_z))
            yield
            for bp, d in ((0, -pair_z), (1, pair_z)):
                arrived(z1.at[ch, bp], p3 + 4 * ch + bp)
                sb[ch, bp] = (wb[ch, bp].astype(F32) + z1[ch, bp].astype(F32)).astype(BF)
                send(sb.at[ch, bp], z2.at[ch, bp], p3 + 4 * ch + 2 + bp, to_z(d))
            yield
            for bp in range(2):
                arrived(z2.at[ch, bp], p3 + 4 * ch + 2 + bp)
            yield from finish(ch, [sb[ch, bp].astype(F32) + z2[ch, bp].astype(F32) for bp in range(2)])

        return [flow(0), flow(1)]

    def pick(shape, kdim):
        k = lax.broadcasted_iota(jnp.int32, shape, kdim)
        m = lax.broadcasted_iota(jnp.int32, shape, 1 - kdim)
        return jnp.where(k == m // 32 * 128 + y * 32 + m % 32, 1.0, 0.0).astype(BF)

    start = gather(va, None, True)
    next(start)
    next(start)
    load_p.wait()
    load_r.wait()
    load_l.wait()
    pick_t = pick((128, 512), 1)
    for t in range(3):
        rsel[pl.ds(128 * t, 128)] = dot(pick_t, rf[t], NT).astype(BF)
    next(start)

    def left_part(cc, bp):
        lrows = jnp.concatenate([lf[t, pl.ds(zl * 128, 128)] for t in range(3)], axis=0)

        def body(k, carry):
            src = [va[:, cc, 2 * k + i, :, bp].reshape(128, 512) for i in range(2)]
            res = dot(lrows, jnp.concatenate(src, axis=0), NT).astype(BF)
            for t in range(3):
                for i in range(2):
                    block = res[128 * t : 128 * t + 128, 128 * i : 128 * i + 128]
                    mid[t, cc * 8 + (2 * k + i) * 2 + bp] = block.reshape(4, 2, 16, 128)
            return carry

        lax.fori_loop(0, 2, body, 0)

    left_part(c, 1)
    next(start)
    left_part(c, 0)
    next(start)
    left_part(1 - c, 1)
    next(start)
    left_part(1 - c, 0)
    pl.semaphore_wait(relay.at[0], 2)

    def pair1(cc, xx):
        rows = []
        for bp in range(2):
            b = cc * 8 + xx * 2 + bp
            rows.append(jnp.concatenate([mid[t, pat[t, b]].reshape(128, 128) for t in range(3)], axis=1))
        res = dot(jnp.concatenate(rows, axis=0), rsel[...], NN)
        return res.reshape(2, 4, 32, 512)

    def finish1(ch, totals):
        rr = lax.broadcasted_iota(jnp.int32, (16, 512), 0) + (zl * 128 + y * 32 + 16 * ch)
        edge = jnp.maximum(rr, lax.broadcasted_iota(jnp.int32, (16, 512), 1))
        for bp in range(2):
            vb[zl, c, x, ch, bp] = jnp.where(edge < sizes[c * 8 + x * 2 + bp], totals[bp], 0.0).astype(BF)
        yield from gather(vb, ch, False)

    flows = reduce(pair1, 16, finish1, *stage1)
    pick_n = pick((512, 128), 0)
    run(flows, 2)
    drain()
    for t in range(3):
        chosen = dot(lf[t], pick_n, NN).astype(BF)
        for zz in range(4):
            for q in range(4):
                for rh in range(2):
                    a = zz * 128 + q * 32 + rh * 16
                    b = q * 128 + rh * 64 + zz * 16
                    lsel[b : b + 16, 128 * t : 128 * t + 128] = chosen[a : a + 16]
    run(flows, 3)

    def right_part(cc, ch):
        rrows = jnp.concatenate([rf[t, pl.ds(zl * 128, 128)] for t in range(3)], axis=0)
        res = dot(vb[:, cc, :, ch].reshape(512, 512), rrows, NT).astype(BF).reshape(4, 8, 16, 384)
        for t in range(3):
            for zz in range(4):
                mid[t, pl.ds(cc * 8, 8), zz, ch] = res[zz, :, :, 128 * t : 128 * t + 128]

    for ch in range(2):
        next(flows[ch])
        right_part(c, ch)
        next(flows[ch])
        right_part(1 - c, ch)
    store = pltpu.make_async_copy(vb.at[zl], out1, lsem.at[5])
    store.start()

    def pair2(cc, xx):
        cols = []
        for bp in range(2):
            b = cc * 8 + xx * 2 + bp
            cols.append(jnp.concatenate([mid[t, pat[t, b]].reshape(128, 128) for t in range(3)], axis=0))
        res = dot(lsel[...], jnp.concatenate(cols, axis=1), NN)
        return jnp.stack([res[:, :128].reshape(4, 128, 128), res[:, 128:].reshape(4, 128, 128)])

    def lanes(zz):
        return pl.ds(pl.multiple_of(zz * 128, 128), 128)

    def finish2(ch, totals):
        shape = (4, 16, 128)
        rr = lax.broadcasted_iota(jnp.int32, shape, 0) * 128 + lax.broadcasted_iota(jnp.int32, shape, 1)
        edge = jnp.maximum(rr + (y * 32 + 16 * ch), lax.broadcasted_iota(jnp.int32, shape, 2) + zl * 128)
        for bp in range(2):
            f2[ch, bp] = jnp.where(edge < sizes[c * 8 + x * 2 + bp], totals[bp].reshape(shape), 0.0).astype(BF)
        here = obuf.at[c, x, ch, :, :, lanes(zl)]
        g2, gc = copies(1), copies(1)
        pltpu.make_async_copy(f2.at[ch, :, zl], here, rsem.at[g2]).start()
        for d in (0, 1, -1, 2 - 4 * ch):
            group = [(f2.at[ch, :, (zl + d + 4) % 4], here, g2, to_xz(dx, d)) for dx in (0, 1, 3, 2) if d or dx]
            send_all(group, f2.at[ch, :, pl.ds(0, len(group))])
        yield
        block = obuf.at[c, :, ch]
        arrived(block, g2)
        send(block, block, gc, other)
        yield
        arrived(obuf.at[1 - c, :, ch], gc)
        yield

    flows = reduce(pair2, 64, finish2, *stage2)
    run(flows, 2)
    drain()
    run(flows, 4)
    drain()
    store.wait()
    assert count[0] == N_ARRIVALS, count


def hand_over(first, second, out1, out2, sem):
    steps = []
    for i, (src, dst) in enumerate(((first, out1), (second, out2))):
        for rh in range(2):
            for bp in range(2):
                steps.append(pltpu.make_async_copy(src.at[:, :, rh, bp], dst.at[:, :, bp, rh], sem.at[i, rh, bp]))
    for step in steps:
        step.start()
    for step in steps:
        step.wait()


def on_device(wave_t, left_ops, right_ops, pattern, sector_size):
    def stage(r, w):
        return [
            pltpu.VMEM((4, 2, 4, 2 * r, w), BF),
            pltpu.VMEM((4, 2, 4, 2 * r, w), BF),
            pltpu.VMEM((4, 2, 2, 4, r, w), BF),
            pltpu.VMEM((2, 3, 4, r, w), BF),
            pltpu.VMEM((2, 3, 4, r, w), BF),
            pltpu.VMEM((2, 3, r, w), BF),
            pltpu.VMEM((2, 4, r, w), F32),
            pltpu.VMEM((2, 3, r, w), BF),
            pltpu.VMEM((2, 3, r, w), BF),
            pltpu.VMEM((2, 3, r, w), BF),
            pltpu.VMEM((2, 2, r, w), BF),
            pltpu.VMEM((2, 2, r, w), BF),
            pltpu.VMEM((2, 2, r, w), BF),
            pltpu.VMEM((2, 2, r, w), BF),
        ]

    hbm = pl.BlockSpec(memory_space=pl.ANY)
    vmem = pl.BlockSpec(memory_space=pltpu.VMEM)
    shape = (2, 4, 2, 2, 16, 512)
    operands = [wave_t.reshape(shape), left_ops, right_ops, pattern, sector_size]
    first, second = pl.pallas_call(
        kernel,
        out_shape=(pltpu.VMEM(shape, BF), pltpu.VMEM(shape, BF)),
        in_specs=[hbm] * 5,
        out_specs=(vmem, vmem),
        scratch_shapes=[
            pltpu.VMEM((2, 4, 2, 2, 16, 512), BF),
            pltpu.VMEM((3, 512, 512), BF),
            pltpu.VMEM((3, 512, 512), BF),
            pltpu.VMEM((384, 512), BF),
            pltpu.VMEM((512, 384), BF),
            pltpu.VMEM((4, 2, 4, 2, 2, 16, 512), BF),
            pltpu.VMEM((4, 2, 4, 2, 2, 16, 512), BF),
            pltpu.VMEM((3, 16, 4, 2, 16, 128), BF),
            pltpu.VMEM((2, 2, 4, 16, 128), BF),
            pltpu.SMEM((3, 16), jnp.int32),
            pltpu.SMEM((16,), jnp.int32),
            pltpu.SemaphoreType.DMA((6,)),
            pltpu.SemaphoreType.DMA((N_SENDS,)),
            pltpu.SemaphoreType.DMA((N_ARRIVALS,)),
            pltpu.SemaphoreType.REGULAR((1,)),
            *stage(16, 512),
            *stage(64, 128),
        ],
        compiler_params=pltpu.CompilerParams(
            collective_id=0, has_side_effects=True, vmem_limit_bytes=40 * 2**20
        ),
        name="hamiltonian",
    )(*[pltpu.with_memory_space_constraint(a, pltpu.HBM) for a in operands])
    result = jax.ShapeDtypeStruct(shape, BF)
    first, second = pl.pallas_call(
        hand_over,
        out_shape=(result, result),
        in_specs=[vmem, vmem],
        out_specs=(hbm, hbm),
        scratch_shapes=[pltpu.SemaphoreType.DMA((2, 2, 2))],
        name="hand_over",
    )(*[pltpu.with_memory_space_constraint(a, pltpu.VMEM) for a in (first, second)])
    return first.reshape(16, 32, 512), second.reshape(16, 32, 512)


def solution(mesh):
    return jax.shard_map(
        on_device,
        mesh=mesh,
        in_specs=(
            P(None, "sec", None),
            P("ops", None, None),
            P("ops", None, None),
            P("ops", None),
            P(),
        ),
        out_specs=(P(None, "sec", None), P(None, "sec", None)),
        check_vma=False,
    )
```

```python
import jax
import jax.numpy as jnp
from jax import lax
from jax.experimental import pallas as pl
from jax.experimental.pallas import tpu as pltpu
from jax.sharding import PartitionSpec as P

MESH = pl.DeviceIdType.MESH
BF = jnp.bfloat16
F32 = jnp.float32
NT = (((1,), (1,)), ((), ()))
NN = (((1,), (0,)), ((), ()))
N_STAGE = 14
N_ARRIVALS = 99
N_SENDS = 60


def dot(a, b, dims):
    return lax.dot_general(a, b, dims, preferred_element_type=F32)


def kernel(wave, lops, rops, pattern, sector, out1, obuf, *scratch):
    wbuf, lf, rf, rsel, lsel, va, vb, mid, f2, pat, sizes, lsem, ssem, rsem, relay = scratch[: -2 * N_STAGE]
    stage1, stage2 = scratch[-2 * N_STAGE : -N_STAGE], scratch[-N_STAGE:]
    ops, sec = lax.axis_index("ops"), lax.axis_index("sec")
    x, zh, c = ops // 8, (ops // 2) % 4, ops % 2
    zl, y = sec // 4, sec % 4
    z = zh * 4 + zl

    def to_x(d):
        return {"ops": ((x + d) % 4 * 4 + zh) * 2 + c, "sec": sec}

    def to_y(d):
        return {"ops": ops, "sec": zl * 4 + (y + d) % 4}

    def to_z(d):
        w = (z + d + 16) % 16
        return {"ops": (x * 4 + w // 4) * 2 + c, "sec": w % 4 * 4 + y}

    def to_xz(dx, d):
        w = (z + d + 16) % 16
        return {"ops": ((x + dx) % 4 * 4 + w // 4) * 2 + c, "sec": w % 4 * 4 + y}

    other = {"ops": ops + 1 - 2 * c, "sec": sec}

    sent = []
    count = [0]

    def copies(n):
        first = count[0]
        count[0] += n
        return first

    def send_all(group, total):
        i = len(sent)
        assert i < N_SENDS, i
        for src, dst, index, device in group:
            pltpu.make_async_remote_copy(
                src_ref=src, dst_ref=dst, send_sem=ssem.at[i], recv_sem=rsem.at[index],
                device_id=device, device_id_type=MESH,
            ).start()
        sent.append(pltpu.make_async_copy(total, total, ssem.at[i]))

    def send(src, dst, index, device):
        send_all([(src, dst, index, device)], src)

    def drain():
        while sent:
            sent.pop().wait()

    def arrived(ref, index):
        pltpu.make_async_copy(ref, ref, rsem.at[index]).wait()

    load_w = pltpu.make_async_copy(wave, wbuf, lsem.at[0])
    load_r = pltpu.make_async_copy(rops, rf, lsem.at[1])
    load_l = pltpu.make_async_copy(lops, lf, lsem.at[2])
    load_s = pltpu.make_async_copy(sector, sizes, lsem.at[3])
    load_p = pltpu.make_async_copy(pattern, pat, lsem.at[4])
    load_w.start()
    load_s.start()
    load_p.start()
    load_r.start()
    load_l.start()
    partners = [other] + [to_y(d) for d in (1, 2, 3)] + [to_x(d) for d in (1, 2, 3)] + [to_z(d) for d in (1, 2, -2, -1)]
    barrier = pltpu.get_barrier_semaphore()
    for device in partners:
        pl.semaphore_signal(barrier, inc=1, device_id=device, device_id_type=MESH)

    load_w.wait()
    load_s.wait()
    row = lax.broadcasted_iota(jnp.int32, (16, 512), 0) + (zl * 128 + y * 32)
    col = lax.broadcasted_iota(jnp.int32, (16, 512), 1)

    def mask_wave(k, carry):
        cc, xx = k // 4, k % 4
        for rh in range(2):
            edge = jnp.maximum(row + 16 * rh, col)
            for bp in range(2):
                block = wbuf[cc, xx, bp, rh].astype(F32)
                va[zl, cc, xx, rh, bp] = jnp.where(edge < sizes[2 * k + bp], block, 0.0).astype(BF)
        return carry

    lax.fori_loop(0, 8, mask_wave, 0)
    pl.semaphore_wait(barrier, len(partners))
    for d in (2, -2):
        pl.semaphore_signal(relay.at[0], inc=1, device_id=to_z(d), device_id_type=MESH)

    z_of = [zl, (zl + 3) % 4, (zl + 1) % 4, (zl + 2) % 4]
    x_of = [x, (x + 3) % 4, (x + 1) % 4, (x + 2) % 4]
    step = [0, 1, 3, 2]

    def gather(v, chunk, whole_slab):
        halves = (0, 1) if chunk is None else (chunk,)
        rows = pl.ds(halves[0], len(halves))
        a1, b1, a2, b2, cx = copies(4), copies(3), copies(4), copies(4), copies(2)

        def z_send(xx, bp, i0):
            block = v.at[zl, c, xx, rows, bp]
            group = []
            for rh in halves:
                part = v.at[zl, c, xx, rh, bp]
                group.append((part, part, i0 + 2 + rh, to_z(2 - 4 * rh)))
            group += [(block, block, i0, to_z(1)), (block, block, i0 + 1, to_z(-1))]
            send_all(group, v.at[zl, c, pl.ds(0, 3), rows, bp])

        def z_arrived(xx, bp, k, i0):
            if k < 3:
                arrived(v.at[z_of[k], c, xx, rows, bp], i0 + k - 1)
            else:
                for rh in halves:
                    arrived(v.at[z_of[k], c, xx, rh, bp], i0 + 2 + rh)

        def x_send(zz, bp, indices):
            block = v.at[zz, c, x, rows, bp]
            group = [(block, block, i, to_x(d)) for d, i in zip((2, 1, 3), (indices[1], indices[0], indices[2]))]
            send_all(group, v.at[zz, c, pl.ds(0, 3), rows, bp])

        z_send(x, 0, a1)
        if whole_slab:
            for k in range(4):
                z_send(x_of[k], 1, b2)
        else:
            x_send(zl, 1, (b1, b1 + 1, b1 + 2))
            x_send(zl, 0, (a2, a2, a2))
            z_send(x, 1, b2)
        yield
        for k in (1, 2, 3):
            if not whole_slab:
                arrived(v.at[zl, c, x_of[k], rows, 1], b1 + step[k] - 1)
                z_send(x_of[k], 1, b2)
            z_arrived(x, 0, k, a1)
            x_send(z_of[k], 0, (a2 + k, a2 + k, a2 + k))
        yield
        if whole_slab:
            for k in (1, 2, 3):
                z_arrived(slice(None), 1, k, b2)
                block = v.at[z_of[k], c, :, :, 1]
                send(block, block, cx, other)
            yield
            for k in (1, 2, 3):
                arrived(v.at[z_of[k], c, pl.ds(0, 3), rows, 0], a2 + k)
                block = v.at[z_of[k], c, :, :, 0]
                send(block, block, cx + 1, other)
            yield
            for i in range(2):
                arrived(v.at[pl.ds(0, 3), 1 - c, :, :, 0], cx + i)
                yield
            return
        for k in range(4):
            arrived(v.at[z_of[k], c, pl.ds(0, 3), rows, 0], a2 + k)
            if k > 0:
                z_arrived(slice(None), 1, k, b2)
            block = v.at[z_of[k], c, :, rows]
            send(block, block, cx, other)
        yield
        arrived(v.at[:, 1 - c, :, rows], cx)
        yield

    def run(flows, steps):
        for _ in range(steps):
            for flow in flows:
                next(flow)

    def reduce(pair, half, finish, s0s, s0r, s0, r1y, r1x, t1, t2, t2b, r2x, r2y, wb, z1, sb, z2):
        pair_z = 4 - 8 * (zh % 2)
        p0, py, px, qx, qy, p3 = copies(4), copies(4), copies(2), copies(2), copies(2), copies(8)
        def theirs(k):
            s0s[k] = pair(1 - c, (x + k + 1) % 4).astype(BF)
            send(s0s.at[k], s0r.at[k], p0 + k, other)

        def first_sends(k, ch):
            if k < 3:
                send(s0.at[k, ch, 1], r1x.at[ch, k], px + ch, to_x(k + 1))
            if k % 2:
                two = pl.ds(k - 1, 2)
                group = [
                    (s0.at[two, ch, 0, (y + e) % 4], r1y.at[ch, e - 1, two], py + 2 * ch + k // 2, to_y(e)) for e in (2, 1, 3)
                ]
                send_all(group, r1y.at[ch, :, two])

        def ours(k):
            total = pair(c, (x + k + 1) % 4)
            arrived(s0r.at[k], p0 + k)
            total = total + s0r[k].astype(F32)
            for ch in range(2):
                for bp in range(2):
                    s0[k, ch, bp] = total[bp, :, ch * half : (ch + 1) * half].astype(BF)
            first_sends(k, 0)

        for k in (0, 1, 2):
            theirs(k)
        ours(0)
        theirs(3)
        for k in (1, 2, 3):
            ours(k)
        for k in range(4):
            first_sends(k, 1)

        def flow(ch):
            def sum_t1(k):
                total = s0[k, ch, 0, y].astype(F32)
                for e in (1, 2, 3):
                    total = total + r1y[ch, e - 1, k].astype(F32)
                return total

            for k in range(4):
                if k % 2 == 0:
                    arrived(r1y.at[ch, :, pl.ds(k, 2)], py + 2 * ch + k // 2)
                if k < 3:
                    t1[ch, k] = sum_t1(k).astype(BF)
                    if k == 2:
                        group = [(t1.at[ch, m], r2x.at[ch, m], qx + ch, to_x(m + 1)) for m in (1, 0, 2)]
                        send_all(group, r2x.at[ch])
            arrived(r1x.at[ch], px + ch)
            mine = s0[3, ch, 1].astype(F32)
            for k in range(3):
                mine = mine + r1x[ch, k].astype(F32)
            t2[ch] = mine
            for e in (1, 2, 3):
                q = (y + e) % 4
                t2b[ch, e - 1] = t2[ch, q].astype(BF)
            group = [(t2b.at[ch, e - 1], r2y.at[ch, e - 1], qy + ch, to_y(e)) for e in (2, 1, 3)]
            send_all(group, r2y.at[ch])
            yield
            w0 = sum_t1(3)
            arrived(r2x.at[ch], qx + ch)
            for k in range(3):
                w0 = w0 + r2x[ch, k].astype(F32)
            wb[ch, 0] = w0.astype(BF)
            send(wb.at[ch, 0], z1.at[ch, 0], p3 + 4 * ch, to_z(pair_z))
            w1 = t2[ch, y]
            arrived(r2y.at[ch], qy + ch)
            for k in range(3):
                w1 = w1 + r2y[ch, k].astype(F32)
            wb[ch, 1] = w1.astype(BF)
            send(wb.at[ch, 1], z1.at[ch, 1], p3 + 4 * ch + 1, to_z(-pair_z))
            yield
            for bp, d in ((0, -pair_z), (1, pair_z)):
                arrived(z1.at[ch, bp], p3 + 4 * ch + bp)
                sb[ch, bp] = (wb[ch, bp].astype(F32) + z1[ch, bp].astype(F32)).astype(BF)
                send(sb.at[ch, bp], z2.at[ch, bp], p3 + 4 * ch + 2 + bp, to_z(d))
            yield
            for bp in range(2):
                arrived(z2.at[ch, bp], p3 + 4 * ch + 2 + bp)
            yield from finish(ch, [sb[ch, bp].astype(F32) + z2[ch, bp].astype(F32) for bp in range(2)])

        return [flow(0), flow(1)]

    def pick(shape, kdim):
        k = lax.broadcasted_iota(jnp.int32, shape, kdim)
        m = lax.broadcasted_iota(jnp.int32, shape, 1 - kdim)
        return jnp.where(k == m // 32 * 128 + y * 32 + m % 32, 1.0, 0.0).astype(BF)

    start = gather(va, None, True)
    next(start)
    next(start)
    load_p.wait()
    load_r.wait()
    load_l.wait()
    pick_t = pick((128, 512), 1)
    for t in range(3):
        rsel[pl.ds(128 * t, 128)] = dot(pick_t, rf[t], NT).astype(BF)
    next(start)

    def left_part(cc, bp):
        lrows = jnp.concatenate([lf[t, pl.ds(zl * 128, 128)] for t in range(3)], axis=0)

        def body(k, carry):
            src = [va[:, cc, 2 * k + i, :, bp].reshape(128, 512) for i in range(2)]
            res = dot(lrows, jnp.concatenate(src, axis=0), NT).astype(BF)
            for t in range(3):
                for i in range(2):
                    block = res[128 * t : 128 * t + 128, 128 * i : 128 * i + 128]
                    mid[t, cc * 8 + (2 * k + i) * 2 + bp] = block.reshape(4, 2, 16, 128)
            return carry

        lax.fori_loop(0, 2, body, 0)

    left_part(c, 1)
    next(start)
    left_part(c, 0)
    next(start)
    left_part(1 - c, 1)
    next(start)
    left_part(1 - c, 0)
    pl.semaphore_wait(relay.at[0], 2)

    def pair1(cc, xx):
        rows = []
        for bp in range(2):
            b = cc * 8 + xx * 2 + bp
            rows.append(jnp.concatenate([mid[t, pat[t, b]].reshape(128, 128) for t in range(3)], axis=1))
        res = dot(jnp.concatenate(rows, axis=0), rsel[...], NN)
        return res.reshape(2, 4, 32, 512)

    def finish1(ch, totals):
        rr = lax.broadcasted_iota(jnp.int32, (16, 512), 0) + (zl * 128 + y * 32 + 16 * ch)
        edge = jnp.maximum(rr, lax.broadcasted_iota(jnp.int32, (16, 512), 1))
        for bp in range(2):
            vb[zl, c, x, ch, bp] = jnp.where(edge < sizes[c * 8 + x * 2 + bp], totals[bp], 0.0).astype(BF)
        yield from gather(vb, ch, False)

    flows = reduce(pair1, 16, finish1, *stage1)
    pick_n = pick((512, 128), 0)
    run(flows, 2)
    drain()
    for t in range(3):
        chosen = dot(lf[t], pick_n, NN).astype(BF)
        for zz in range(4):
            for q in range(4):
                for rh in range(2):
                    a = zz * 128 + q * 32 + rh * 16
                    b = q * 128 + rh * 64 + zz * 16
                    lsel[b : b + 16, 128 * t : 128 * t + 128] = chosen[a : a + 16]
    run(flows, 3)

    def right_part(cc, ch):
        rrows = jnp.concatenate([rf[t, pl.ds(zl * 128, 128)] for t in range(3)], axis=0)
        res = dot(vb[:, cc, :, ch].reshape(512, 512), rrows, NT).astype(BF).reshape(4, 8, 16, 384)
        for t in range(3):
            for zz in range(4):
                mid[t, pl.ds(cc * 8, 8), zz, ch] = res[zz, :, :, 128 * t : 128 * t + 128]

    for ch in range(2):
        next(flows[ch])
        right_part(c, ch)
        next(flows[ch])
        right_part(1 - c, ch)
    store = pltpu.make_async_copy(vb.at[zl], out1, lsem.at[5])
    store.start()

    def pair2(cc, xx):
        cols = []
        for bp in range(2):
            b = cc * 8 + xx * 2 + bp
            cols.append(jnp.concatenate([mid[t, pat[t, b]].reshape(128, 128) for t in range(3)], axis=0))
        res = dot(lsel[...], jnp.concatenate(cols, axis=1), NN)
        return jnp.stack([res[:, :128].reshape(4, 128, 128), res[:, 128:].reshape(4, 128, 128)])

    def lanes(zz):
        return pl.ds(pl.multiple_of(zz * 128, 128), 128)

    def finish2(ch, totals):
        shape = (4, 16, 128)
        rr = lax.broadcasted_iota(jnp.int32, shape, 0) * 128 + lax.broadcasted_iota(jnp.int32, shape, 1)
        edge = jnp.maximum(rr + (y * 32 + 16 * ch), lax.broadcasted_iota(jnp.int32, shape, 2) + zl * 128)
        for bp in range(2):
            f2[ch, bp] = jnp.where(edge < sizes[c * 8 + x * 2 + bp], totals[bp].reshape(shape), 0.0).astype(BF)
        here = obuf.at[c, x, ch, :, :, lanes(zl)]
        g2, gc = copies(1), copies(1)
        pltpu.make_async_copy(f2.at[ch, :, zl], here, rsem.at[g2]).start()
        for d in (2 - 4 * ch, 1, -1, 0):
            group = [(f2.at[ch, :, (zl + d + 4) % 4], here, g2, to_xz(dx, d)) for dx in (2, 1, 3, 0) if d or dx]
            send_all(group, f2.at[ch, :, pl.ds(0, len(group))])
        yield
        block = obuf.at[c, :, ch]
        arrived(block, g2)
        send(block, block, gc, other)
        yield
        arrived(obuf.at[1 - c, :, ch], gc)
        yield

    flows = reduce(pair2, 64, finish2, *stage2)
    run(flows, 2)
    drain()
    run(flows, 4)
    drain()
    store.wait()
    assert count[0] == N_ARRIVALS, count


def hand_over(first, second, out1, out2, sem):
    steps = []
    for i, (src, dst) in enumerate(((first, out1), (second, out2))):
        for rh in range(2):
            for bp in range(2):
                steps.append(pltpu.make_async_copy(src.at[:, :, rh, bp], dst.at[:, :, bp, rh], sem.at[i, rh, bp]))
    for step in steps:
        step.start()
    for step in steps:
        step.wait()


def on_device(wave_t, left_ops, right_ops, pattern, sector_size):
    def stage(r, w):
        return [
            pltpu.VMEM((4, 2, 4, 2 * r, w), BF),
            pltpu.VMEM((4, 2, 4, 2 * r, w), BF),
            pltpu.VMEM((4, 2, 2, 4, r, w), BF),
            pltpu.VMEM((2, 3, 4, r, w), BF),
            pltpu.VMEM((2, 3, 4, r, w), BF),
            pltpu.VMEM((2, 3, r, w), BF),
            pltpu.VMEM((2, 4, r, w), F32),
            pltpu.VMEM((2, 3, r, w), BF),
            pltpu.VMEM((2, 3, r, w), BF),
            pltpu.VMEM((2, 3, r, w), BF),
            pltpu.VMEM((2, 2, r, w), BF),
            pltpu.VMEM((2, 2, r, w), BF),
            pltpu.VMEM((2, 2, r, w), BF),
            pltpu.VMEM((2, 2, r, w), BF),
        ]

    hbm = pl.BlockSpec(memory_space=pl.ANY)
    vmem = pl.BlockSpec(memory_space=pltpu.VMEM)
    shape = (2, 4, 2, 2, 16, 512)
    operands = [wave_t.reshape(shape), left_ops, right_ops, pattern, sector_size]
    first, second = pl.pallas_call(
        kernel,
        out_shape=(pltpu.VMEM(shape, BF), pltpu.VMEM(shape, BF)),
        in_specs=[hbm] * 5,
        out_specs=(vmem, vmem),
        scratch_shapes=[
            pltpu.VMEM((2, 4, 2, 2, 16, 512), BF),
            pltpu.VMEM((3, 512, 512), BF),
            pltpu.VMEM((3, 512, 512), BF),
            pltpu.VMEM((384, 512), BF),
            pltpu.VMEM((512, 384), BF),
            pltpu.VMEM((4, 2, 4, 2, 2, 16, 512), BF),
            pltpu.VMEM((4, 2, 4, 2, 2, 16, 512), BF),
            pltpu.VMEM((3, 16, 4, 2, 16, 128), BF),
            pltpu.VMEM((2, 2, 4, 16, 128), BF),
            pltpu.SMEM((3, 16), jnp.int32),
            pltpu.SMEM((16,), jnp.int32),
            pltpu.SemaphoreType.DMA((6,)),
            pltpu.SemaphoreType.DMA((N_SENDS,)),
            pltpu.SemaphoreType.DMA((N_ARRIVALS,)),
            pltpu.SemaphoreType.REGULAR((1,)),
            *stage(16, 512),
            *stage(64, 128),
        ],
        compiler_params=pltpu.CompilerParams(
            collective_id=0, has_side_effects=True, vmem_limit_bytes=40 * 2**20
        ),
        name="hamiltonian",
    )(*[pltpu.with_memory_space_constraint(a, pltpu.HBM) for a in operands])
    result = jax.ShapeDtypeStruct(shape, BF)
    first, second = pl.pallas_call(
        hand_over,
        out_shape=(result, result),
        in_specs=[vmem, vmem],
        out_specs=(hbm, hbm),
        scratch_shapes=[pltpu.SemaphoreType.DMA((2, 2, 2))],
        name="hand_over",
    )(*[pltpu.with_memory_space_constraint(a, pltpu.VMEM) for a in (first, second)])
    return first.reshape(16, 32, 512), second.reshape(16, 32, 512)


def solution(mesh):
    return jax.shard_map(
        on_device,
        mesh=mesh,
        in_specs=(
            P(None, "sec", None),
            P("ops", None, None),
            P("ops", None, None),
            P("ops", None),
            P(),
        ),
        out_specs=(P(None, "sec", None), P(None, "sec", None)),
        check_vma=False,
    )
```
